32 devices in a mesh: seq: 8 (over z, y), state: 4 (over x, core).
Axes of the slice: x: 2, y: 2, z: 4, core: 2. Of those that a mesh axis runs over, the one named last changes fastest.
Arguments:
- inputs: bfloat16 [2048, 16, 512], P('state', 'seq'), may hold values from -6 to 6
- lengths: int32 [16], P('seq'), may hold values from 256 to 2048, as said below
- norm_gain: float32 [2, 512], replicated, may hold values from 0.25 to 1.75
- norm_bias: float32 [2, 512], replicated, may hold values from -3 to 3
- in_proj: bfloat16 [2, 2, 512, 256], P(None, None, None, 'state'), may hold values from -0.1875 to 0.1875
- out_proj: bfloat16 [2, 2, 256, 512], P(None, None, 'state'), may hold values from -0.375 to 0.375
- nu_log: float32 [2, 256], P(None, 'state'), may hold values from -9.5 to -3
- theta_log: float32 [2, 256], P(None, 'state'), may hold values from -6.9 to -0.5
- gamma_gain: float32 [2, 256], P(None, 'state'), may hold values from 0.25 to 1.75
- skip_gain: float32 [2, 512], replicated, may hold values from -4 to 4
- glu_weight: bfloat16 [2, 512, 1024], replicated, may hold values from -0.25 to 0.25
- cotangent: bfloat16 [2048, 16, 512], P('state', 'seq'), may hold values from -6 to 6
Outputs:
- outputs: float32 [2048, 16, 512], P('state', 'seq')
- input_grad: float32 [2048, 16, 512], P('state', 'seq')
- norm_gain_grad: float32 [2, 512], replicated
- norm_bias_grad: float32 [2, 512], replicated
- in_proj_grad: float32 [2, 2, 512, 256], P(None, None, None, 'state')
- out_proj_grad: float32 [2, 2, 256, 512], P(None, None, 'state')
- nu_grad: float32 [2, 256], P(None, 'state')
- theta_grad: float32 [2, 256], P(None, 'state')
- gamma_grad: float32 [2, 256], P(None, 'state')
- skip_grad: float32 [2, 512], replicated
- glu_grad: float32 [2, 512, 1024], replicated
The draws below stay inside these ranges and needn't reach their ends.
Inputs may be any that keep to these rules, and one draw needn't show every extreme that they name: `lengths`: in every aligned group of 2 sequences at least one has length 2048.
All inputs are finite; a program needn't handle non-finite values.
Results may differ from the reference program's by a relative error of at most 0.02.
The reference program's roundings to bfloat16 on the way count: a program that leaves them out, or rounds other values in their place, can miss the bound.
Values may be sent and summed in bfloat16 or wider, within the bound.
A program may use at most 256 MiB of HBM per device.

```python
import jax
import jax.numpy as jnp
from jax import lax

D = 512
N = 256
LEN = 2048
SEQ_DEV = 2
LAYERS = 2
SEQS = 16


def draw_lengths(key, part):
    key = jax.random.fold_in(key, 11)
    first_key, second_key = jax.random.split(key)
    groups = SEQS // SEQ_DEV
    drawn = jax.random.randint(first_key, (groups, SEQ_DEV), LEN // 8, LEN + 1)
    chosen = jax.random.randint(second_key, (groups, 1), 0, SEQ_DEV)
    longest = jnp.arange(SEQ_DEV)[None, :] == chosen
    return jnp.where(longest, LEN, drawn).reshape(SEQS).astype(jnp.int32)


def block_levels(stream_key, extent, pieces, low, top_value):
    def one(axis_at, shards_of):
        steps = jax.random.uniform(jax.random.fold_in(jax.random.fold_in(stream_key, 6), axis_at), (shards_of,), jnp.float32, low / len(pieces), top_value / len(pieces))
        return jnp.repeat(jnp.exp(steps), extent[axis_at] // shards_of).reshape((-1,) + (1,) * (len(extent) - axis_at - 1))

    loudness = one(*pieces[0])
    for cut in pieces[1:]:
        loudness = loudness * one(*cut)
    return loudness


def normal_values(stream_key, shape, spread, limit, pieces=(), held_as=jnp.bfloat16):
    array = jax.random.normal(stream_key, shape, jnp.float32) * spread
    if len(pieces) > 0:
        array = block_levels(stream_key, shape, pieces, -0.22, 0.18) * array
    return jnp.clip(array, min=-limit, max=limit).astype(held_as)


def setup_inputs(seed: int = 0) -> dict:
    splits = jax.random.split(jax.random.key(seed), 13)
    return {
        "inputs": normal_values(splits[0], (LEN, SEQS, D), 1.0, 6.0, ((0, 4), (1, 8))),
        "lengths": draw_lengths(jax.random.fold_in(splits[12], 71), 0),
        "norm_gain": jnp.clip(1.0 + 0.15 * jax.random.normal(splits[2], (LAYERS, D), jnp.float32), 0.25, 1.75),
        "norm_bias": normal_values(splits[3], (LAYERS, D), 0.5, 3.0, (), jnp.float32),
        "in_proj": normal_values(splits[4], (LAYERS, 2, D, N), (2 * D) ** -0.5, 0.1875, ((3, 4),)),
        "out_proj": normal_values(splits[5], (LAYERS, 2, N, D), N ** -0.5, 0.375, ((2, 4),)),
        "nu_log": jnp.clip(-9.5 + 6.5 * jax.random.uniform(splits[6], (LAYERS, N), jnp.float32) ** block_levels(splits[6], (LAYERS, N), ((1, 4),), -0.2, 0.2), -9.5, -3.0),
        "theta_log": jnp.clip(-6.9 + 6.4 * jax.random.uniform(splits[7], (LAYERS, N), jnp.float32) ** block_levels(splits[7], (LAYERS, N), ((1, 4),), -0.2, 0.2), -6.9, -0.5),
        "gamma_gain": jnp.clip(1.0 + 0.15 * jax.random.normal(splits[8], (LAYERS, N), jnp.float32), 0.25, 1.75),
        "skip_gain": normal_values(splits[9], (LAYERS, D), 1.0, 4.0, (), jnp.float32),
        "glu_weight": normal_values(splits[10], (LAYERS, D, 2 * D), D ** -0.5, 0.25),
        "cotangent": normal_values(splits[11], (LEN, SEQS, D), 1.0, 6.0, ((0, 4), (1, 8))),
    }


EPSILON = 1e-05
HIGHEST = lax.Precision.HIGHEST

@jax.custom_vjp
def low(v):
    return lax.optimization_barrier(v.astype(jnp.bfloat16)).astype(jnp.float32)

@jax.custom_vjp
def low_back(v):
    return v

def low_keep(v):
    return (low(v), None)

def low_pass(kept, grad):
    return (grad,)

def back_keep(v):
    return (v, None)

def back_low(kept, grad):
    return (low(grad),)
low.defvjp(low_keep, low_pass)
low_back.defvjp(back_keep, back_low)

def combine_steps(earlier, later):
    are_one, aim_one, bre_one, bim_one = earlier
    are_two, aim_two, bre_two, bim_two = later
    return (are_two * are_one - aim_two * aim_one, are_two * aim_one + aim_two * are_one, are_two * bre_one - aim_two * bim_one + bre_two, are_two * bim_one + aim_two * bre_one + bim_two)

def recurrence(projected, nu_param, theta_param, gamma_param, validity, backward_in_time):
    rate = jnp.exp(nu_param)
    modulus = jnp.exp(-rate)
    phase = jnp.exp(theta_param)
    scaled = gamma_param * jnp.sqrt(-jnp.expm1(-2.0 * rate))
    keep_mask = validity[..., None]
    step_real = keep_mask * (modulus * jnp.cos(phase)) + (1.0 - keep_mask)
    step_imag = keep_mask * (modulus * jnp.sin(phase))
    input_real = projected[..., 0, :] * scaled * keep_mask
    input_imag = projected[..., 1, :] * scaled * keep_mask
    scanned = lax.associative_scan(combine_steps, (step_real, step_imag, input_real, input_imag), reverse=backward_in_time, axis=0)
    return jnp.stack([scanned[2], scanned[3]], axis=-2)

def block_forward(activations, validity, layer_gain, layer_bias, in_weight, out_weight, nu_param, theta_param, gamma_param, layer_skip, glu_matrix, backward_in_time):
    weights_mask = validity[..., None]
    count = jnp.sum(validity)
    feature_mean = lax.optimization_barrier(jnp.sum(weights_mask * activations, axis=(0, 1))) / count
    centered = activations - feature_mean
    variance = lax.optimization_barrier(jnp.sum(weights_mask * centered * centered, axis=(0, 1))) / count
    inverse_std = lax.rsqrt(variance + EPSILON)
    signed_out = jnp.concatenate([out_weight[0], -out_weight[1]], axis=0)
    width = activations.shape[-1]

    def one_sequence(pair):
        sequence, valid_seq = pair
        normed = (sequence - feature_mean) * inverse_std * layer_gain + layer_bias
        rounded = low(normed)
        projected = low_back(jnp.einsum('ld,cdn->lcn', rounded, in_weight, precision=HIGHEST))
        states = recurrence(projected, nu_param, theta_param, gamma_param, valid_seq, backward_in_time)
        flat_states = low(states.reshape(states.shape[0], -1))
        mixed = low_back(jnp.dot(flat_states, signed_out, precision=HIGHEST))
        pre_act = mixed + layer_skip * normed
        hidden = low(jax.nn.gelu(pre_act))
        both = low_back(jnp.dot(hidden, glu_matrix, precision=HIGHEST))
        return sequence + both[:, :width] * jax.nn.sigmoid(both[:, width:])
    return lax.map(jax.checkpoint(one_sequence), (activations, validity))

def reference(inputs, lengths, norm_gain, norm_bias, in_proj, out_proj, nu_log, theta_log, gamma_gain, skip_gain, glu_weight, cotangent):
    positions = jnp.arange(LEN, dtype=jnp.int32)
    validity = (positions[None, :] < lengths[:, None]).astype(jnp.float32)
    start_acts = jnp.swapaxes(inputs.astype(jnp.float32), 0, 1)
    params = tuple((weight_item.astype(jnp.float32) for weight_item in (norm_gain, norm_bias, in_proj, out_proj, nu_log, theta_log, gamma_gain, skip_gain, glu_weight)))

    def forward(activations, gains, biases, in_weights, out_weights, nus, thetas, gammas, skips, glus):
        for depth_index in range(LAYERS):
            activations = block_forward(activations, validity, gains[depth_index], biases[depth_index], in_weights[depth_index], out_weights[depth_index], nus[depth_index], thetas[depth_index], gammas[depth_index], skips[depth_index], glus[depth_index], depth_index % 2 == 1)
        return activations
    result, pullback = jax.vjp(forward, start_acts, *params)
    gradients = pullback(jnp.swapaxes(cotangent.astype(jnp.float32), 0, 1))
    return (jnp.swapaxes(result, 0, 1), jnp.swapaxes(gradients[0], 0, 1), gradients[1], gradients[2], gradients[3], gradients[4], gradients[5], gradients[6], gradients[7], gradients[8], gradients[9])
```

```python
import math

import jax
import jax.numpy as jnp
from jax import lax
from jax.experimental import pallas as pl
from jax.experimental.pallas import tpu as pltpu
from jax.sharding import PartitionSpec as P

EPSILON = 1e-05
MESH = pl.DeviceIdType.MESH
F32 = jnp.float32
BF16 = jnp.bfloat16
CHUNKS = 16
GELU_A = math.sqrt(2.0 / math.pi)
GELU_B = 0.044715
VMEM_LIMIT = 63 * 2**20


def dot_nn(a, b):
    return lax.dot_general(a, b, (((1,), (0,)), ((), ())), preferred_element_type=F32)


def dot_nt(a, b):
    return lax.dot_general(a, b, (((1,), (1,)), ((), ())), preferred_element_type=F32)


def dot_tn(a, b):
    return lax.dot_general(a, b, (((0,), (0,)), ((), ())), preferred_element_type=F32)


class Buffers:
    def __init__(self):
        self.shapes = []

    def add(self, shape, dtype):
        self.shapes.append(pltpu.VMEM(shape, dtype))
        return len(self.shapes) - 1

    def bind(self, refs):
        bound = Buffers()
        for key, places in vars(self).items():
            if places is not self.shapes:
                setattr(bound, key, jax.tree.map(lambda i: refs[i], places))
        return bound


def build(axis_seq, axis_state, rows, seqs, width, states_own, layers):
    NS, NT = axis_seq, axis_state
    N = NS * NT
    NX = NT // 2
    NY = NX if NS % NX == 0 else 1
    NZ = NS // NY
    L, Q, D, NL = rows, seqs, width, states_own
    ST = L // CHUNKS
    SN = NL * NT
    SL2 = 2 * SN
    E = 2 * D
    T = Q * L
    RT = min(256, L)
    TILES = L // RT
    UN = 4
    assert layers == 2 and NT % 2 == 0 and L % CHUNKS == 0

    v = Buffers()
    vm = v.add
    v.x0 = vm((T, D), BF16)
    v.cot = vm((T, D), BF16)
    v.u1 = vm((T, D), F32)
    v.mask = vm((T, 128), F32)
    v.nlow, v.slow, v.hid = ([vm((T, D), BF16) for _ in range(2)] for _ in range(3))
    v.proj = [vm((T, SL2), F32) for _ in range(2)]
    v.state = [vm((Q, (ST + 1) * CHUNKS, SL2), F32) for _ in range(2)]
    v.apow = [vm((Q, 2, CHUNKS, SN), F32) for _ in range(2)]
    v.cin = [vm((Q, 2, CHUNKS, SL2), F32) for _ in range(2)]
    v.win, v.wout = ([vm((2, NT, NL, D), BF16) for _ in range(2)] for _ in range(2))
    v.st_msg, v.sm_msg = ([vm((4, D), F32) for _ in range(2)] for _ in range(2))
    v.st_buf, v.sm_buf = ([vm((N, 4, D), F32) for _ in range(2)] for _ in range(2))
    v.bw_msg = [vm((2, D), F32) for _ in range(2)]
    v.bw_buf = [vm((N, 2, D), F32) for _ in range(2)]
    v.stat, v.small = ([vm((8, D), F32) for _ in range(2)] for _ in range(2))
    v.ca_msg = [[[vm((2, SL2), F32) for _ in range(Q)] for _ in range(2)] for _ in range(2)]
    v.ca_buf = [[[vm((NT, 2, SL2), F32) for _ in range(Q)] for _ in range(2)] for _ in range(2)]
    v.dgelu, v.lin, v.gate, v.preg, v.up = (vm((T, D), F32) for _ in range(5))
    v.wglu = vm((2, D, E), BF16)
    v.bothg = vm((T, E), BF16)
    v.mlow = vm((T, D), BF16)
    v.sgrad = vm((T, SL2), F32)
    v.par_buf = vm((NT, 8, SN), F32)
    v.par = vm((8, SN), F32)
    v.full = vm((SN, D), F32)

    def reduce_buffers(rr, cc, whole):
        h = rr // 2
        hx = h // NX
        hy = hx // NY
        cz = cc // NZ if (cc // NZ) % 128 == 0 else cc
        return [
            vm((h, cc), F32),
            [vm((h, cc), BF16), vm((NX, hx, cc), BF16), vm((NY, hy, cc), BF16), vm((NZ, hy, cz), BF16)],
            [vm((h, cc), BF16), vm((NX, hx, cc), BF16), vm((NY, hy, cc), BF16), vm((NZ, hy, cz), BF16)],
            vm((rr if whole else hx, cc), BF16),
        ]

    kinds = [(D, E, True), (SL2, D, False), (SL2, D, False)]
    v.red = [[reduce_buffers(*kind) for kind in kinds] for _ in range(2)]
    places = v
    SEMS = 160
    scratch = v.shapes + [
        pltpu.SemaphoreType.DMA((SEMS,)),
        pltpu.SemaphoreType.DMA((SEMS,)),
        pltpu.SemaphoreType.DMA((SEMS,)),
    ]

    def kernel(
        x_hbm, cot_hbm, len_ref, nrm_ref, par_ref, win_hbm, wout_hbm, glu_hbm,
        u2_out, ig_out, small_out, int_out, out_out, glu_out, *rest,
    ):
        v = places.bind(rest[: len(places.shapes)])
        ssem, rsem, lsem = rest[len(places.shapes):]
        me_s, me_t = lax.axis_index("seq"), lax.axis_index("state")
        me = me_s * NT + me_t
        core, mx = lax.rem(me_t, 2), me_t // 2
        my, mz = lax.rem(me_s, NY), me_s // NY
        CORE = (2, core, lambda p: (me_s, mx * 2 + p))
        X = (NX, mx, lambda p: (me_s, p * 2 + core))
        Y = (NY, my, lambda p: (mz * NY + p, me_t))
        Z = (NZ, mz, lambda p: (p * NY + my, me_t))
        STATE = (NT, me_t, lambda p: (me_s, p))
        ALL = (N, me, lambda p: (p // NT, lax.rem(p, NT)))
        remotes, locals_, pending = [], [], []

        def once(wait):
            left = [wait]
            pending.append(lambda: left.pop()() if left else None)
            return pending[-1]

        def wait_bytes(view, sem):
            pltpu.make_async_copy(view, view, sem).wait()

        def send(axis, src_of, dst_of, size_view):
            n, coord, dev = axis
            k = len(remotes)
            remotes.append(k)
            assert k < SEMS
            if n == 1:
                return lambda: None

            def one(step):
                p = lax.rem(coord + step, n)
                pltpu.make_async_remote_copy(
                    src_ref=src_of(p), dst_ref=dst_of(coord), send_sem=ssem.at[k],
                    recv_sem=rsem.at[k], device_id=dev(p), device_id_type=MESH,
                ).start()

            if n <= 8:
                for step in range(1, n):
                    one(step)
            else:
                def body(step, c):
                    one(step)
                    return c
                lax.fori_loop(1, n, body, 0)
            once(lambda: wait_bytes(size_view(n - 1), ssem.at[k]))
            return once(lambda: wait_bytes(size_view(n - 1), rsem.at[k]))

        def load(src, dst):
            k = len(locals_)
            locals_.append(k)
            copy = pltpu.make_async_copy(src, dst, lsem.at[k])
            copy.start()
            return once(copy.wait)

        got_x = load(x_hbm, v.x0)
        got_own = [load(win_hbm.at[0], v.win[0].at[:, me_t]), load(wout_hbm.at[0], v.wout[0].at[:, me_t])]
        got_glu = load(glu_hbm, v.wglu)
        got_cot = load(cot_hbm, v.cot)

        barrier = pltpu.get_barrier_semaphore()

        def greet(step, c):
            p = lax.rem(me + step, N)
            pl.semaphore_signal(barrier, inc=1, device_id=(p // NT, lax.rem(p, NT)), device_id_type=MESH)
            return c

        lax.fori_loop(1, N, greet, 0)

        base = me_t * L
        row = lax.broadcasted_iota(jnp.int32, (L, 128), 0)
        token = base + lax.rem(row, CHUNKS) * ST + row // CHUNKS
        count_own = jnp.float32(0)
        for q in range(Q):
            v.mask[q * L:(q + 1) * L, :] = (token < len_ref[q]).astype(F32)
            count_own = count_own + jnp.clip(len_ref[q] - base, 0, L).astype(F32)

        pl.semaphore_wait(barrier, N - 1)

        v.par_buf[me_t] = par_ref[...]
        got_par = send(STATE, lambda p: par_ref, lambda c: v.par_buf.at[c], lambda n: v.par_buf.at[pl.ds(0, n)])

        def gather_weight(hbm, l, dst):
            return send(
                STATE, lambda p: hbm.at[l], lambda c: dst.at[:, c],
                lambda n: dst.at[:, pl.ds(0, n)],
            )

        got_win = [gather_weight(win_hbm, 0, v.win[0]), None]
        got_wout = [gather_weight(wout_hbm, 0, v.wout[0]), None]

        def start_layer1_weights():
            got_own.append(load(win_hbm.at[1], v.win[1].at[:, me_t]))
            got_own.append(load(wout_hbm.at[1], v.wout[1].at[:, me_t]))
            got_win[1] = gather_weight(win_hbm, 1, v.win[1])
            got_wout[1] = gather_weight(wout_hbm, 1, v.wout[1])

        def rep(m, w=D):
            return jnp.concatenate([m] * (w // 128), axis=1)

        def tiles(body, init, count=T // RT):
            return lax.fori_loop(0, count, lambda i, c: body(pl.multiple_of(i * RT, RT), c), init)

        def fold8(a):
            return jnp.sum(a.reshape(a.shape[0] // 8, 8, a.shape[1]), axis=0)

        def fold1(a):
            return jnp.sum(a, axis=0, keepdims=True)

        zero8 = jnp.zeros((8, D), F32)

        def local_stats(read, l, total=None):
            if total is None:
                def add(r, acc):
                    return acc + fold8(read(r) * rep(v.mask[pl.ds(r, RT), :]))
                total = tiles(add, zero8)
            mean_own = fold1(total) / jnp.maximum(count_own, 1.0)

            def spread(r, acc):
                c = read(r) - mean_own
                return acc + fold8(c * c * rep(v.mask[pl.ds(r, RT), :]))

            squares = fold1(tiles(spread, zero8))
            v.st_msg[l][0:1, :] = mean_own
            v.st_msg[l][1:2, :] = squares
            v.st_msg[l][2:3, :] = jnp.full((1, D), 1.0, F32) * count_own
            v.st_msg[l][3:4, :] = jnp.zeros((1, D), F32)
            v.st_buf[l][me] = v.st_msg[l][...]
            return send(
                ALL, lambda p: v.st_msg[l], lambda c: v.st_buf[l].at[c],
                lambda n: v.st_buf[l].at[pl.ds(0, n)],
            )

        def global_stats(l, got):
            got()
            buf = v.st_buf[l]
            means, squares, counts = buf[:, 0:1, :], buf[:, 1:2, :], buf[:, 2:3, :]
            count = jnp.sum(counts, axis=0)
            mean = jnp.sum(means * counts, axis=0) / count
            off = means - mean[None]
            variance = jnp.sum(squares + counts * off * off, axis=0) / count
            stat = v.stat[l]
            stat[0:1, :] = mean
            stat[1:2, :] = lax.rsqrt(variance + EPSILON)
            stat[2:3, :] = count

        def normalise(l, u):
            stat = v.stat[l]
            standard = (u - stat[0:1, :]) * stat[1:2, :]
            return standard, standard * nrm_ref[3 * l:3 * l + 1, :] + nrm_ref[3 * l + 1:3 * l + 2, :]

        def read_u(l):
            if l == 0:
                return lambda r: v.x0[pl.ds(r, RT), :].astype(F32)
            return lambda r: v.u1[pl.ds(r, RT), :]

        def valid_count(q):
            chunk = lax.broadcasted_iota(jnp.int32, (CHUNKS, SN), 0)
            return jnp.clip(len_ref[q] - base - chunk * ST, 0, ST)

        def lam(l):
            return v.par[3 * l:3 * l + 1, :], v.par[3 * l + 1:3 * l + 2, :], v.par[3 * l + 2:3 * l + 3, :]

        def chunk_powers(l):
            for q in range(Q):
                nv = valid_count(q)
                lre, lim, _ = lam(l)
                lre = jnp.broadcast_to(lre, (CHUNKS, SN))
                lim = jnp.broadcast_to(lim, (CHUNKS, SN))
                pre, pim = jnp.ones((CHUNKS, SN), F32), jnp.zeros((CHUNKS, SN), F32)
                bit = 1
                while bit <= ST:
                    on = (nv & bit) != 0
                    nre, nim = pre * lre - pim * lim, pre * lim + pim * lre
                    pre, pim = jnp.where(on, nre, pre), jnp.where(on, nim, pim)
                    lre, lim = lre * lre - lim * lim, 2.0 * lre * lim
                    bit *= 2
                v.apow[l][q, 0] = pre
                v.apow[l][q, 1] = pim

        def steps(body, init, reverse):
            def outer(i, c):
                for j in range(UN):
                    s = i * UN + j
                    if reverse:
                        s = ST - 1 - s
                    c = body(s, c)
                return c
            return lax.fori_loop(0, ST // UN, outer, init)

        def at_step(q, s):
            return pl.ds(pl.multiple_of(q * L + s * CHUNKS, CHUNKS), CHUNKS)

        def chunk_scan(q, l, end_re, end_im, conj, reverse):
            are, aim = v.apow[l][q, 0], v.apow[l][q, 1]
            if conj:
                aim = -aim
            ere, eim = end_re, end_im
            chunk = lax.broadcasted_iota(jnp.int32, (CHUNKS, SN), 0)

            def shifted(a, d, fill):
                if reverse:
                    return jnp.where(chunk < CHUNKS - d, pltpu.roll(a, CHUNKS - d, 0), fill)
                return jnp.where(chunk >= d, pltpu.roll(a, d, 0), fill)

            d = 1
            while d < CHUNKS:
                sre, sim = shifted(ere, d, 0.0), shifted(eim, d, 0.0)
                tre, tim = shifted(are, d, 1.0), shifted(aim, d, 0.0)
                ere, eim = are * sre - aim * sim + ere, are * sim + aim * sre + eim
                are, aim = are * tre - aim * tim, are * tim + aim * tre
                d *= 2
            edge = 0 if reverse else CHUNKS - 1
            total = [a[edge:edge + 1, :] for a in (ere, eim, are, aim)]
            enter = [shifted(ere, 1, 0.0), shifted(eim, 1, 0.0), shifted(are, 1, 1.0), shifted(aim, 1, 0.0)]
            return enter, total

        def send_carry(l, way, q, enter, total):
            msg, buf = v.ca_msg[l][way][q], v.ca_buf[l][way][q]
            msg[0:1, 0:SN] = total[0]
            msg[0:1, SN:] = total[1]
            msg[1:2, 0:SN] = total[2]
            msg[1:2, SN:] = total[3]
            v.cin[l][q, 0, :, 0:SN] = enter[0]
            v.cin[l][q, 0, :, SN:] = enter[1]
            v.cin[l][q, 1, :, 0:SN] = enter[2]
            v.cin[l][q, 1, :, SN:] = enter[3]
            buf[me_t] = msg[...]
            return send(STATE, lambda p: msg, lambda c: buf.at[c], lambda n: buf.at[pl.ds(0, n)])

        def take_carry(l, way, q, got, reverse):
            got()
            buf = v.ca_buf[l][way][q]
            cre, cim = jnp.zeros((1, SN), F32), jnp.zeros((1, SN), F32)
            for j in (range(NT - 1, -1, -1) if reverse else range(NT)):
                before = (j > me_t) if reverse else (j < me_t)
                ere, eim = buf[j, 0:1, 0:SN], buf[j, 0:1, SN:]
                are, aim = buf[j, 1:2, 0:SN], buf[j, 1:2, SN:]
                nre, nim = are * cre - aim * cim + ere, are * cim + aim * cre + eim
                cre, cim = jnp.where(before, nre, cre), jnp.where(before, nim, cim)
            cin = v.cin[l]
            ere, eim = cin[q, 0, :, 0:SN], cin[q, 0, :, SN:]
            are, aim = cin[q, 1, :, 0:SN], cin[q, 1, :, SN:]
            return ere + are * cre - aim * cim, eim + are * cim + aim * cre

        def forward_step(l, q, nv, s, c):
            lre, lim, scale = lam(l)
            here = at_step(q, s)
            bre = v.proj[l][here, 0:SN] * scale
            bim = v.proj[l][here, SN:] * scale
            keep = s < nv
            cre, cim = c
            nre, nim = lre * cre - lim * cim + bre, lre * cim + lim * cre + bim
            return jnp.where(keep, nre, cre), jnp.where(keep, nim, cim)

        def scan_ends(l, q):
            reverse = l % 2 == 1
            nv = valid_count(q)
            zero = jnp.zeros((CHUNKS, SN), F32)
            ere, eim = steps(lambda s, c: forward_step(l, q, nv, s, c), (zero, zero), reverse)
            enter, total = chunk_scan(q, l, ere, eim, False, reverse)
            return send_carry(l, 0, q, enter, total)

        def scan_states(l, q, got):
            reverse = l % 2 == 1
            nv = valid_count(q)
            init = take_carry(l, 0, q, got, reverse)
            state, low = v.state[l], v.slow[l]
            edge = ST if reverse else 0
            state[q, edge * CHUNKS:(edge + 1) * CHUNKS, 0:SN] = init[0]
            state[q, edge * CHUNKS:(edge + 1) * CHUNKS, SN:] = init[1]

            def body(s, c):
                nre, nim = forward_step(l, q, nv, s, c)
                at = pl.ds(pl.multiple_of((s if reverse else s + 1) * CHUNKS, CHUNKS), CHUNKS)
                state[q, at, 0:SN] = nre
                state[q, at, SN:] = nim
                here = at_step(q, s)
                low[here, 0:SN] = nre.astype(BF16)
                low[here, SN:] = nim.astype(BF16)
                return nre, nim

            steps(body, init, reverse)

        def adjoint_step(l, q, nv, s, c):
            lre, lim, _ = lam(l)
            here = at_step(q, s)
            are = v.sgrad[here, 0:SN] + c[0]
            aim = v.sgrad[here, SN:] + c[1]
            keep = s < nv
            nre, nim = lre * are + lim * aim, lre * aim - lim * are
            return (are, aim), keep, (jnp.where(keep, nre, are), jnp.where(keep, nim, aim))

        def adjoint_ends(l, q):
            reverse = l % 2 == 0
            nv = valid_count(q)
            zero = jnp.zeros((CHUNKS, SN), F32)
            ere, eim = steps(lambda s, c: adjoint_step(l, q, nv, s, c)[2], (zero, zero), reverse)
            enter, total = chunk_scan(q, l, ere, eim, True, reverse)
            return send_carry(l, 1, q, enter, total)

        def adjoint_states(l, q, got, sums):
            reverse = l % 2 == 0
            nv = valid_count(q)
            init = take_carry(l, 1, q, got, reverse)
            state, proj = v.state[l], v.proj[l]
            _, _, scale = lam(l)

            def body(s, c):
                w, (gre, gim, gsc) = c
                (are, aim), keep, w = adjoint_step(l, q, nv, s, w)
                are, aim = jnp.where(keep, are, 0.0), jnp.where(keep, aim, 0.0)
                here = at_step(q, s)
                v.mlow[here, 0:SN] = (are * scale).astype(BF16)
                v.mlow[here, SN:] = (aim * scale).astype(BF16)
                at = pl.ds(pl.multiple_of((s if reverse else s + 1) * CHUNKS, CHUNKS), CHUNKS)
                pre, pim = state[q, at, 0:SN], state[q, at, SN:]
                gre = gre + are * pre + aim * pim
                gim = gim + aim * pre - are * pim
                gsc = gsc + are * proj[here, 0:SN] + aim * proj[here, SN:]
                return w, (gre, gim, gsc)

            return steps(body, (init, sums), reverse)[1]

        class Reduce:
            def __init__(self, refs, rr, cc, whole):
                self.own, self.s, self.r, self.res = refs
                self.cc, self.whole = cc, whole
                self.h = rr // 2
                self.hx = self.h // NX
                self.hy = self.hx // NY
                self.split = (cc // NZ) % 128 == 0
                self.cz = cc // NZ if self.split else cc
                self.stage = 0
                self.got = None

            def start(self):
                self.got = send(CORE, lambda p: self.s[0], lambda c: self.r[0], lambda n: self.r[0])

            def row_level(self, axis, n, coord, piece, base, s, r):
                for k in range(1, n):
                    p = lax.rem(coord + k, n)
                    s[p] = self.own[pl.ds(pl.multiple_of(base + p * piece, 8), piece), :].astype(BF16)
                return send(axis, lambda p: s.at[p], lambda c: r.at[c], lambda m: r.at[pl.ds(0, m)])

            def gather(self, n, coord, piece, base, r):
                base = base + coord * piece
                at = pl.ds(pl.multiple_of(base, 8), piece)
                total = self.own[at, :]
                for k in range(1, n):
                    total = total + r[lax.rem(coord + k, n)].astype(F32)
                self.own[at, :] = total
                return base

            def where(self, cols=None):
                if self.whole:
                    r0 = core * self.h + mx * self.hx + my * self.hy
                else:
                    r0 = my * self.hy
                r0 = pl.multiple_of(r0, 8)
                if cols is None:
                    return self.res.at[pl.ds(r0, self.hy), :]
                return self.res.at[pl.ds(r0, self.hy), pl.ds(pl.multiple_of(cols * self.cz, 128), self.cz)]

            def block(self, rows, r0):
                return self.res.at[pl.ds(pl.multiple_of(r0, 8), rows), :]

            def step(self):
                k = self.stage
                self.stage += 1
                if k <= 7 and self.got is not None:
                    self.got()
                    self.got = None
                if k == 0:
                    h, own = self.h, self.own
                    own[...] = own[...] + self.r[0][...].astype(F32)
                    self.base = 0
                    self.got = self.row_level(X, NX, mx, self.hx, 0, self.s[1], self.r[1])
                elif k == 1:
                    self.base = self.gather(NX, mx, self.hx, 0, self.r[1])
                    self.got = self.row_level(Y, NY, my, self.hy, self.base, self.s[2], self.r[2])
                elif k == 2:
                    self.base = self.gather(NY, my, self.hy, self.base, self.r[2])
                    s, r = self.s[3], self.r[3]
                    mine = pl.ds(pl.multiple_of(self.base, 8), self.hy)
                    if self.split:
                        for p in range(NZ):
                            s[p] = self.own[mine, p * self.cz:(p + 1) * self.cz].astype(BF16)
                        self.got = send(Z, lambda p: s.at[p], lambda c: r.at[c], lambda m: r.at[pl.ds(0, m)])
                    else:
                        s[0] = self.own[mine, :].astype(BF16)
                        r[mz] = s[0]
                        self.got = send(Z, lambda p: s.at[0], lambda c: r.at[c], lambda m: r.at[pl.ds(0, m)])
                elif k == 3:
                    r = self.r[3]
                    if self.split:
                        at = pl.ds(pl.multiple_of(mz * self.cz, 128), self.cz)
                        total = self.own[pl.ds(pl.multiple_of(self.base, 8), self.hy), at]
                        for j in range(1, NZ):
                            total = total + r[lax.rem(mz + j, NZ)].astype(F32)
                        spot = self.where(mz)
                        spot[...] = total.astype(BF16)
                        self.got = send(Z, lambda p: spot, lambda c: self.where(c), lambda m: r.at[pl.ds(0, m)])
                    else:
                        total = r[0].astype(F32)
                        for j in range(1, NZ):
                            total = total + r[j].astype(F32)
                        self.where()[...] = total.astype(BF16)
                        self.got = None
                elif k == 4:
                    spot = self.where()
                    self.got = send(Y, lambda p: spot, lambda c: spot, lambda m: self.r[2].at[pl.ds(0, m)])
                elif k == 5 and self.whole:
                    spot = self.block(self.hx, core * self.h + mx * self.hx)
                    self.got = send(X, lambda p: spot, lambda c: spot, lambda m: self.r[1].at[pl.ds(0, m)])
                elif k == 6 and self.whole:
                    spot = self.block(self.h, core * self.h)
                    self.got = send(CORE, lambda p: spot, lambda c: spot, lambda m: self.r[0])

            last = 8

        reducers = [[Reduce(v.red[l][k], *kinds[k]) for k in range(3)] for l in range(2)]

        def glu_gradient(l):
            red = reducers[l][0]
            h = D // 2
            for which in (0, 1):
                at = pl.ds(pl.multiple_of((core if which else 1 - core) * h, 128), h)
                part = dot_tn(v.hid[l][:, at], v.bothg[...])
                if which:
                    red.own[...] = part
                else:
                    red.s[0][...] = part.astype(BF16)
                    red.start()

        def state_matrix_gradient(red, left, right):
            for c in range(2):
                v.full[...] = dot_tn(left[:, c * SN:(c + 1) * SN], right[...])
                for x in range(NX):
                    dst = pl.ds((x * 2 + c) * NL, NL)
                    mine = pl.ds(pl.multiple_of(x * 2 * NL + core * NL, 8), NL)
                    theirs = pl.ds(pl.multiple_of(x * 2 * NL + (1 - core) * NL, 8), NL)
                    red.s[0][dst, :] = v.full[theirs, :].astype(BF16)
                    red.own[dst, :] = v.full[mine, :]
            red.start()

        def weight(ref):
            return ref[...].reshape(SL2, D)

        def forward_tile(l, r):
            at = pl.ds(r, RT)
            u = read_u(l)(r)
            _, normed = normalise(l, u)
            mixed = dot_nn(v.slow[l][at, :], weight(v.wout[l]))
            x = mixed + nrm_ref[3 * l + 2:3 * l + 3, :] * normed
            x2 = x * x
            t = jnp.tanh(x * (GELU_A + (GELU_A * GELU_B) * x2))
            half = 0.5 * (1.0 + t)
            hidden = (x * half).astype(BF16)
            v.hid[l][at, :] = hidden
            dgelu = half + (0.5 * x) * (1.0 - t * t) * (GELU_A + (3.0 * GELU_A * GELU_B) * x2)
            both = dot_nn(hidden, v.wglu[l])
            linear = both[:, :D]
            gate = 0.5 + 0.5 * jnp.tanh(0.5 * both[:, D:])
            return u, normed, dgelu, linear, gate

        def backward_tile(l, r, upstream, normed, dgelu, linear, gate):
            at = pl.ds(r, RT)
            pass_gate = upstream * gate
            bothg = jnp.concatenate([pass_gate, pass_gate * linear * (1.0 - gate)], axis=1).astype(BF16)
            v.bothg[at, :] = bothg
            preg = dot_nt(bothg, v.wglu[l]) * dgelu
            v.preg[at, :] = preg
            mlow = preg.astype(BF16)
            v.mlow[at, :] = mlow
            v.sgrad[at, :] = dot_nt(mlow, weight(v.wout[l]))
            return fold8(preg * normed)

        def norm_grads(l, q, sums):
            def body(r, c):
                at = pl.ds(r + q * L, RT)
                standard, _ = normalise(l, read_u(l)(r + q * L))
                ng = v.preg[at, :] * nrm_ref[3 * l + 2:3 * l + 3, :] + dot_nn(v.mlow[at, :], weight(v.win[l]))
                v.preg[at, :] = ng
                return c[0] + fold8(ng), c[1] + fold8(ng * standard)
            return tiles(body, sums, TILES)

        def send_norm_grads(l, sums):
            msg, buf = v.bw_msg[l], v.bw_buf[l]
            msg[0:1, :] = fold1(sums[0])
            msg[1:2, :] = fold1(sums[1])
            buf[me] = msg[...]
            return send(ALL, lambda p: msg, lambda c: buf.at[c], lambda n: buf.at[pl.ds(0, n)])

        def send_small(l, skip, chain):
            msg, buf = v.sm_msg[l], v.sm_buf[l]
            msg[0:1, :] = fold1(skip)
            msg[1:2, 0:SN] = fold1(chain[0])
            msg[1:2, SN:] = fold1(chain[1])
            msg[2:3, 0:SN] = fold1(chain[2])
            msg[2:3, SN:] = jnp.zeros((1, SN), F32)
            msg[3:4, :] = jnp.zeros((1, D), F32)
            buf[me] = msg[...]
            return send(ALL, lambda p: msg, lambda c: buf.at[c], lambda n: buf.at[pl.ds(0, n)])

        def take_norm_grads(l, got):
            got()
            buf = v.bw_buf[l]
            total = jnp.sum(buf[...], axis=0)
            v.small[l][0:2, :] = total

        def take_small(l, got):
            got()
            total = jnp.sum(v.sm_buf[l][...], axis=0)
            v.small[l][2:6, :] = total
            v.small[l][6:8, :] = jnp.zeros((2, D), F32)

        def input_gradient(l, r, upstream):
            stat, small = v.stat[l], v.small[l]
            standard, _ = normalise(l, read_u(l)(r))
            m = rep(v.mask[pl.ds(r, RT), :])
            inner = small[0:1, :] + standard * small[1:2, :]
            ng = v.preg[pl.ds(r, RT), :] - m * inner / stat[2:3, :]
            return upstream + stat[1:2, :] * nrm_ref[3 * l:3 * l + 1, :] * ng

        got_x()
        got = local_stats(read_u(0), 0)
        got_par()
        v.par[...] = jnp.sum(v.par_buf[...], axis=0)
        chunk_powers(0)
        chunk_powers(1)
        for w in got_own:
            w()
        got_own.clear()
        global_stats(0, got)
        start_layer1_weights()

        def project(l, q):
            def body(r, c):
                at = pl.ds(r + q * L, RT)
                _, normed = normalise(l, read_u(l)(r + q * L))
                low = normed.astype(BF16)
                v.nlow[l][at, :] = low
                v.proj[l][at, :] = dot_nt(low, weight(v.win[l]))
                return c
            tiles(body, 0, TILES)

        def forward_scan(l):
            got_win[l]()
            waits = []
            for q in range(Q):
                project(l, q)
                waits.append(scan_ends(l, q))
            got_wout[l]()
            v.wout[l][1] = -v.wout[l][1]
            return waits

        waits = forward_scan(0)
        got_glu()
        total = zero8
        for q in range(Q):
            scan_states(0, q, waits[q])

            def body(r, acc, q=q):
                at = pl.ds(r + q * L, RT)
                u, normed, dgelu, linear, gate = forward_tile(0, r + q * L)
                v.dgelu[at, :] = dgelu
                v.lin[at, :] = linear
                v.gate[at, :] = gate
                u = u + linear * gate
                v.u1[at, :] = u
                return acc + fold8(u * rep(v.mask[at, :]))

            total = tiles(body, total, TILES)

        got = local_stats(read_u(1), 1, total)
        for w in got_own:
            w()
        got_own.clear()
        global_stats(1, got)
        waits = forward_scan(1)
        got_cot()
        skip = zero8
        waits_b = []
        for q in range(Q):
            scan_states(1, q, waits[q])

            def body(r, acc, q=q):
                at = pl.ds(r + q * L, RT)
                u, normed, dgelu, linear, gate = forward_tile(1, r + q * L)
                v.up[at, :] = u + linear * gate
                upstream = v.cot[at, :].astype(F32)
                return acc + backward_tile(1, r + q * L, upstream, normed, dgelu, linear, gate)

            skip = tiles(body, skip, TILES)
            waits_b.append(adjoint_ends(1, q))
        stored = [load(v.up, u2_out)]

        def finish_backward(l, waits_b, skip, before, between):
            glu_gradient(l)
            state_matrix_gradient(reducers[l][1], v.slow[l], v.mlow)
            before()
            chain = (jnp.zeros((CHUNKS, SN), F32),) * 3
            sums = (zero8, zero8)
            for q in range(Q):
                chain = adjoint_states(l, q, waits_b[q], chain)
                sums = norm_grads(l, q, sums)
            got = send_norm_grads(l, sums)
            state_matrix_gradient(reducers[l][2], v.mlow, v.nlow[l])
            got_small = send_small(l, skip, chain)
            between()
            take_norm_grads(l, got)
            return got_small

        def advance(*which):
            for red in which:
                red.step()

        (g0, o0, i0), (g1, o1, i1) = reducers
        got_small1 = finish_backward(1, waits_b, skip, lambda: None, lambda: advance(g1, o1))
        stored[0]()

        skip = zero8
        waits_b = []
        for q in range(Q):
            def body(r, acc, q=q):
                at = pl.ds(r + q * L, RT)
                upstream = input_gradient(1, r + q * L, v.cot[at, :].astype(F32))
                v.up[at, :] = upstream
                _, normed = normalise(0, read_u(0)(r + q * L))
                return acc + backward_tile(0, r + q * L, upstream, normed, v.dgelu[at, :], v.lin[at, :], v.gate[at, :])

            skip = tiles(body, skip, TILES)
            if q == 0:
                advance(g1, o1, i1)
            waits_b.append(adjoint_ends(0, q))
        advance(g1, o1, i1)
        got_small0 = finish_backward(
            0, waits_b, skip, lambda: advance(g1, o1, i1), lambda: advance(g1, o1, i1, g0, o0))

        def body(r, c):
            at = pl.ds(r, RT)
            v.up[at, :] = input_gradient(0, r, v.up[at, :])
            return c

        tiles(body, 0)
        stored = [load(v.up, ig_out)]
        take_small(1, got_small1)
        take_small(0, got_small0)
        for l in range(2):
            stored.append(load(v.small[l], small_out.at[l]))
        order = [g1, g0, o1, o0, i1, i0]
        while any(red.stage < Reduce.last for red in order):
            for red in sorted(order, key=lambda red: red.stage):
                if red.stage < Reduce.last:
                    red.step()
        for l in range(2):
            stored.append(load(reducers[l][0].res, glu_out.at[l]))
            stored.append(load(reducers[l][1].res, out_out.at[l]))
            stored.append(load(reducers[l][2].res, int_out.at[l]))
        for w in pending:
            w()

    out_shape = [
        jax.ShapeDtypeStruct((T, D), F32),
        jax.ShapeDtypeStruct((T, D), F32),
        jax.ShapeDtypeStruct((2, 8, D), F32),
        jax.ShapeDtypeStruct((2, 2 * NL, D), BF16),
        jax.ShapeDtypeStruct((2, 2 * NL, D), BF16),
        jax.ShapeDtypeStruct((2, D, E), BF16),
    ]
    hbm = pl.BlockSpec(memory_space=pl.ANY)
    vmem = pl.BlockSpec(memory_space=pltpu.VMEM)
    smem = pl.BlockSpec(memory_space=pltpu.SMEM)
    return pl.pallas_call(
        kernel,
        out_shape=out_shape,
        in_specs=[hbm, hbm, smem, vmem, vmem, hbm, hbm, hbm],
        out_specs=[hbm] * 6,
        scratch_shapes=scratch,
        compiler_params=pltpu.CompilerParams(
            collective_id=0, has_side_effects=True, vmem_limit_bytes=VMEM_LIMIT
        ),
    )


def solution(mesh):
    seq_devices, state_devices = mesh.shape["seq"], mesh.shape["state"]

    def per_device(
        inputs, lengths, norm_gain, norm_bias, in_proj, out_proj,
        nu_log, theta_log, gamma_gain, skip_gain, glu_weight, cotangent,
    ):
        rows, seqs, width = inputs.shape
        layers, own = nu_log.shape
        steps = rows // CHUNKS
        states = own * state_devices
        place = lax.axis_index("state")

        def by_chunks(a):
            a = a.reshape(CHUNKS, steps, seqs, width).transpose(2, 1, 0, 3)
            return a.reshape(seqs * rows, width)

        def by_tokens(a):
            a = a.reshape(seqs, steps, CHUNKS, width).transpose(2, 1, 0, 3)
            return a.reshape(rows, seqs, width)

        rate = jnp.exp(nu_log)
        modulus = jnp.exp(-rate)
        phase = jnp.exp(theta_log)
        lam_re, lam_im = modulus * jnp.cos(phase), modulus * jnp.sin(phase)
        root = jnp.sqrt(-jnp.expm1(-2.0 * rate))
        scale = gamma_gain * root
        params = jnp.stack([lam_re, lam_im, scale], axis=1).reshape(3 * layers, own)
        params = jnp.concatenate([params, jnp.zeros((8 - 3 * layers, own), F32)], axis=0)
        mine = jnp.arange(states, dtype=jnp.int32) // own == place
        params = jnp.where(mine, jnp.tile(params, (1, state_devices)), 0.0)
        norm_rows = jnp.stack([norm_gain, norm_bias, skip_gain], axis=1).reshape(3 * layers, width)
        norm_rows = jnp.concatenate([norm_rows, jnp.zeros((8 - 3 * layers, width), F32)], axis=0)

        call = build(seq_devices, state_devices, rows, seqs, width, own, layers)
        u2, input_grad, small, in_grad, out_grad, glu_grad = call(
            by_chunks(inputs), by_chunks(cotangent), lengths, norm_rows, params,
            jnp.swapaxes(in_proj, 2, 3), out_proj, glu_weight,
        )
        at = place * own
        sum_re = lax.dynamic_slice_in_dim(small[:, 3, :states], at, own, axis=1)
        sum_im = lax.dynamic_slice_in_dim(small[:, 3, states:], at, own, axis=1)
        sum_sc = lax.dynamic_slice_in_dim(small[:, 4, :states], at, own, axis=1)
        rate_grad = -(sum_re * lam_re + sum_im * lam_im) + sum_sc * gamma_gain * jnp.exp(-2.0 * rate) / root
        phase_grad = sum_im * lam_re - sum_re * lam_im
        in_grad = in_grad.astype(F32).reshape(layers, 2, own, width)
        out_grad = out_grad.astype(F32).reshape(layers, 2, own, width)
        sign = jnp.array([1.0, -1.0], F32).reshape(1, 2, 1, 1)
        return (
            by_tokens(u2),
            by_tokens(input_grad),
            small[:, 1],
            small[:, 0],
            jnp.swapaxes(in_grad, 2, 3),
            out_grad * sign,
            rate * rate_grad,
            phase * phase_grad,
            sum_sc * root,
            small[:, 2],
            glu_grad.astype(F32),
        )

    return jax.shard_map(
        per_device,
        mesh=mesh,
        in_specs=(
            P("state", "seq", None),
            P("seq"),
            P(),
            P(),
            P(None, None, None, "state"),
            P(None, None, "state", None),
            P(None, "state"),
            P(None, "state"),
            P(None, "state"),
            P(),
            P(),
            P("state", "seq", None),
        ),
        out_specs=(
            P("state", "seq", None),
            P("state", "seq", None),
            P(),
            P(),
            P(None, None, None, "state"),
            P(None, None, "state", None),
            P(None, "state"),
            P(None, "state"),
            P(None, "state"),
            P(),
            P(),
        ),
        check_vma=False,
    )
```

```python
import math

import jax
import jax.numpy as jnp
from jax import lax
from jax.experimental import pallas as pl
from jax.experimental.pallas import tpu as pltpu
from jax.sharding import PartitionSpec as P

EPSILON = 1e-05
MESH = pl.DeviceIdType.MESH
F32 = jnp.float32
BF16 = jnp.bfloat16
CHUNKS = 16
GELU_A = math.sqrt(2.0 / math.pi)
GELU_B = 0.044715
VMEM_LIMIT = 65280 * 1024


def dot_nn(a, b):
    return lax.dot_general(a, b, (((1,), (0,)), ((), ())), preferred_element_type=F32)


def dot_nt(a, b):
    return lax.dot_general(a, b, (((1,), (1,)), ((), ())), preferred_element_type=F32)


def dot_tn(a, b):
    return lax.dot_general(a, b, (((0,), (0,)), ((), ())), preferred_element_type=F32)


class Buffers:
    def __init__(self):
        self.shapes = []

    def add(self, shape, dtype):
        self.shapes.append(pltpu.VMEM(shape, dtype))
        return len(self.shapes) - 1

    def bind(self, refs):
        bound = Buffers()
        for key, places in vars(self).items():
            if places is not self.shapes:
                setattr(bound, key, jax.tree.map(lambda i: refs[i], places))
        return bound


def build(axis_seq, axis_state, rows, seqs, width, states_own, layers):
    NS, NT = axis_seq, axis_state
    N = NS * NT
    NX = NT // 2
    NY = NX if NS % NX == 0 else 1
    NZ = NS // NY
    L, Q, D, NL = rows, seqs, width, states_own
    ST = L // CHUNKS
    SN = NL * NT
    SL2 = 2 * SN
    E = 2 * D
    T = Q * L
    RT = min(512, L)
    TILES = L // RT
    UN = 4
    assert layers == 2 and NT % 2 == 0 and L % CHUNKS == 0

    v = Buffers()
    vm = v.add
    LT = D // 128
    FLAT = T * LT
    v.raw = vm((FLAT, 128), BF16)
    v.flat = vm((FLAT, 128), F32)
    v.x0 = vm((T, D), BF16)
    v.cot = vm((T, D), BF16)
    v.u1 = vm((T, D), F32)
    v.mask = vm((T, 128), F32)
    v.nlow, v.slow, v.hid = ([vm((T, D), BF16) for _ in range(2)] for _ in range(3))
    v.proj = [vm((T, SL2), F32) for _ in range(2)]
    v.state = [vm((Q, (ST + 1) * CHUNKS, SL2), F32) for _ in range(2)]
    v.apow = [vm((Q, 2, CHUNKS, SN), F32) for _ in range(2)]
    v.cin = [vm((Q, 2, CHUNKS, SL2), F32) for _ in range(2)]
    v.win, v.wout = ([vm((2, NT, NL, D), BF16) for _ in range(2)] for _ in range(2))
    v.st_msg, v.bw_msg = ([vm((2, D), F32) for _ in range(2)] for _ in range(2))
    v.st_buf, v.bw_buf = ([vm((N, 2, D), F32) for _ in range(2)] for _ in range(2))
    v.len_msg = vm((8, 128), F32)
    v.len_buf = vm((NS, 8, 128), F32)
    v.sm_msg = vm((8, D), F32)
    v.sm_buf = vm((NT, 8, D), F32)
    v.sm_sum = vm((8, D), F32)
    v.sm_all = vm((NS, 8, D), F32)
    v.stat, v.small = ([vm((8, D), F32) for _ in range(2)] for _ in range(2))
    v.ca_msg = [[[vm((2, SL2), F32) for _ in range(Q)] for _ in range(2)] for _ in range(2)]
    v.ca_buf = [[[vm((NT, 2, SL2), F32) for _ in range(Q)] for _ in range(2)] for _ in range(2)]
    v.dgelu, v.lin, v.gate, v.preg, v.up = (vm((T, D), F32) for _ in range(5))
    v.wglu = vm((2, D, E), BF16)
    v.bothg = vm((T, E), BF16)
    v.mlow = vm((T, D), BF16)
    v.sgrad = vm((T, SL2), F32)
    v.par_msg = vm((8, 128), F32)
    v.par_buf = vm((NT, 8, 128), F32)
    v.par = vm((8, SN), F32)
    v.result = vm((16, D), F32)
    v.counts = vm((N, 1, D), F32)
    v.full = vm((SN, D), F32)

    def reduce_buffers(rr, cc, whole, turned):
        h = rr // 2
        n1, n2 = (NY, NX) if turned else (NX, NY)
        p1 = h // n1
        p2 = p1 // n2
        p3 = p2 // NZ
        last = (NZ - 1, p3, cc) if p3 % 16 == 0 else (NZ, p2, cc)
        return [
            vm((h, cc), F32),
            vm((h, cc), BF16),
            [vm((1, h, cc), BF16), vm((max(n1 - 1, 1), p1, cc), BF16), vm((max(n2 - 1, 1), p2, cc), BF16), vm(last, BF16)],
            vm((rr if whole else 2 * NL, cc), BF16),
        ]

    kinds = [(D, E // 2, True), (SL2, D // 2, False), (SL2, D // 2, False)]
    v.red = [[[reduce_buffers(*kind, turned) for turned in (False, True)] for kind in kinds] for _ in range(2)]
    places = v
    SEMS = 160
    scratch = v.shapes + [
        pltpu.SemaphoreType.DMA((SEMS,)),
        pltpu.SemaphoreType.DMA((SEMS,)),
        pltpu.SemaphoreType.DMA((SEMS,)),
    ]

    def kernel(
        x_hbm, cot_hbm, len_ref, gain_ref, bias_ref, nu_ref, theta_ref, gamma_ref, skip_ref, win_hbm, wout_hbm, glu_hbm,
        u2_out, ig_out, small_out, int_out, out_out, glu_out, *rest,
    ):
        v = places.bind(rest[: len(places.shapes)])
        ssem, rsem, lsem = rest[len(places.shapes):]
        me_s, me_t = lax.axis_index("seq"), lax.axis_index("state")
        me = me_s * NT + me_t
        core, mx = lax.rem(me_t, 2), me_t // 2
        my, mz = lax.rem(me_s, NY), me_s // NY
        CORE = (2, core, lambda p: (me_s, mx * 2 + p))
        X = (NX, mx, lambda p: (me_s, p * 2 + core))
        Y = (NY, my, lambda p: (mz * NY + p, me_t))
        Z = (NZ, mz, lambda p: (p * NY + my, me_t))
        STATE = (NT, me_t, lambda p: (me_s, p))
        SEQ = (NS, me_s, lambda p: (p, me_t))
        ALL = (N, me, lambda p: (p // NT, lax.rem(p, NT)))
        remotes, locals_, pending = [], [], []

        def once(wait):
            left = [wait]
            pending.append(lambda: left.pop()() if left else None)
            return pending[-1]

        def wait_bytes(view, sem):
            pltpu.make_async_copy(view, view, sem).wait()

        def exchange(axis, src_of, dst_of, size_view):
            n, coord, dev = axis
            k = len(remotes)
            remotes.append(k)
            assert k < SEMS
            if n == 1:
                return once(lambda: None), once(lambda: None)

            def one(step):
                p = lax.rem(coord + step, n)
                pltpu.make_async_remote_copy(
                    src_ref=src_of(p, step), dst_ref=dst_of(coord, step), send_sem=ssem.at[k],
                    recv_sem=rsem.at[k], device_id=dev(p), device_id_type=MESH,
                ).start()

            if n <= 8:
                for step in range(1, n):
                    one(step)
            else:
                def body(step, c):
                    one(step)
                    return c
                lax.fori_loop(1, n, body, 0)
            return (
                once(lambda: wait_bytes(size_view(n - 1), rsem.at[k])),
                once(lambda: wait_bytes(size_view(n - 1), ssem.at[k])),
            )

        def send(axis, src, buf):
            return exchange(axis, lambda p, k: src, lambda c, k: buf.at[c], lambda n: buf.at[pl.ds(0, n)])[0]

        def load(src, dst):
            k = len(locals_)
            locals_.append(k)
            copy = pltpu.make_async_copy(src, dst, lsem.at[k])
            copy.start()
            return once(copy.wait)

        got_x = load(x_hbm, v.raw)
        got_own = [load(hbm.at[l], dst[l].at[:, me_t]) for l in range(2) for hbm, dst in ((win_hbm, v.win), (wout_hbm, v.wout))]
        got_glu = load(glu_hbm, v.wglu)

        barrier = pltpu.get_barrier_semaphore()

        def greet(step, c):
            p = lax.rem(me + step, N)
            pl.semaphore_signal(barrier, inc=1, device_id=(p // NT, lax.rem(p, NT)), device_id_type=MESH)
            return c

        lax.fori_loop(1, N, greet, 0)

        class Gather:
            def __init__(self, dst):
                self.dst = dst
                self.x = self.spread(X, me_t)
                self.rest = [self.spread(CORE, me_t)]

            def spread(self, axis, slot):
                spot = self.dst.at[:, slot]
                return exchange(axis, lambda p, k: spot, lambda c, k: spot, lambda n: self.dst.at[:, pl.ds(0, n)])

            def relay(self):
                self.x[0]()
                self.rest += [self.spread(CORE, lax.rem(mx + k, NX) * 2 + core) for k in range(1, NX)]

            def take(self):
                self.x[1]()
                for came, sent in self.rest:
                    came()
                    sent()

        def rep(m, w=D):
            return jnp.concatenate([m] * (w // 128), axis=1)

        def tiles(body, init, count=T // RT):
            return lax.fori_loop(0, count, lambda i, c: body(pl.multiple_of(i * RT, RT), c), init)

        def fold8(a):
            return jnp.sum(a.reshape(a.shape[0] // 8, 8, a.shape[1]), axis=0)

        def fold1(a):
            return jnp.sum(a, axis=0, keepdims=True)

        zero8 = jnp.zeros((8, D), F32)

        def local_stats(read, l, total=None):
            if total is None:
                def add(r, acc):
                    return acc + fold8(read(r) * rep(v.mask[pl.ds(r, RT), :]))
                total = tiles(add, zero8)
            mean_own = fold1(total) / jnp.maximum(count_own, 1.0)

            def spread(r, acc):
                c = read(r) - mean_own
                return acc + fold8(c * c * rep(v.mask[pl.ds(r, RT), :]))

            squares = fold1(tiles(spread, zero8))
            v.st_msg[l][0:1, :] = mean_own
            v.st_msg[l][1:2, :] = squares
            v.st_buf[l][me] = v.st_msg[l][...]

        def global_stats(l, got):
            got()
            buf = v.st_buf[l]
            means, squares = buf[:, 0:1, :], buf[:, 1:2, :]
            counts = v.counts[...]
            count = jnp.sum(counts, axis=0)
            mean = jnp.sum(means * counts, axis=0) / count
            off = means - mean[None]
            variance = jnp.sum(squares + counts * off * off, axis=0) / count
            stat = v.stat[l]
            stat[0:1, :] = mean
            stat[1:2, :] = lax.rsqrt(variance + EPSILON)
            stat[2:3, :] = count

        def take_counts():
            got_len()
            for s in range(NS):
                for t in range(NT):
                    held = jnp.zeros((1, 128), F32)
                    for q in range(Q):
                        held = held + jnp.clip(v.len_buf[s, q:q + 1, :] - float(t * L), 0.0, float(L))
                    v.counts[s * NT + t] = rep(held)

        def normalise(l, u):
            stat = v.stat[l]
            standard = (u - stat[0:1, :]) * stat[1:2, :]
            return standard, standard * gain_ref[l:l + 1, :] + bias_ref[l:l + 1, :]

        def read_u(l):
            if l == 0:
                return lambda r: v.x0[pl.ds(r, RT), :].astype(F32)
            return lambda r: v.u1[pl.ds(r, RT), :]

        def valid_count(q):
            chunk = lax.broadcasted_iota(jnp.int32, (CHUNKS, SN), 0)
            return jnp.clip(len_ref[q] - base - chunk * ST, 0, ST)

        def lam(l):
            return v.par[3 * l:3 * l + 1, :], v.par[3 * l + 1:3 * l + 2, :], v.par[3 * l + 2:3 * l + 3, :]

        def chunk_powers(l):
            for q in range(Q):
                nv = valid_count(q)
                lre, lim, _ = lam(l)
                lre = jnp.broadcast_to(lre, (CHUNKS, SN))
                lim = jnp.broadcast_to(lim, (CHUNKS, SN))
                pre, pim = jnp.ones((CHUNKS, SN), F32), jnp.zeros((CHUNKS, SN), F32)
                bit = 1
                while bit <= ST:
                    on = (nv & bit) != 0
                    nre, nim = pre * lre - pim * lim, pre * lim + pim * lre
                    pre, pim = jnp.where(on, nre, pre), jnp.where(on, nim, pim)
                    lre, lim = lre * lre - lim * lim, 2.0 * lre * lim
                    bit *= 2
                v.apow[l][q, 0] = pre
                v.apow[l][q, 1] = pim

        def steps(body, init, reverse):
            def outer(i, c):
                for j in range(UN):
                    s = i * UN + j
                    if reverse:
                        s = ST - 1 - s
                    c = body(s, c)
                return c
            return lax.fori_loop(0, ST // UN, outer, init)

        def at_step(q, s):
            return pl.ds(pl.multiple_of(q * L + s * CHUNKS, CHUNKS), CHUNKS)

        def chunk_scan(q, l, end_re, end_im, conj, reverse):
            are, aim = v.apow[l][q, 0], v.apow[l][q, 1]
            if conj:
                aim = -aim
            ere, eim = end_re, end_im
            chunk = lax.broadcasted_iota(jnp.int32, (CHUNKS, SN), 0)

            def shifted(a, d, fill):
                if reverse:
                    return jnp.where(chunk < CHUNKS - d, pltpu.roll(a, CHUNKS - d, 0), fill)
                return jnp.where(chunk >= d, pltpu.roll(a, d, 0), fill)

            d = 1
            while d < CHUNKS:
                sre, sim = shifted(ere, d, 0.0), shifted(eim, d, 0.0)
                tre, tim = shifted(are, d, 1.0), shifted(aim, d, 0.0)
                ere, eim = are * sre - aim * sim + ere, are * sim + aim * sre + eim
                are, aim = are * tre - aim * tim, are * tim + aim * tre
                d *= 2
            edge = 0 if reverse else CHUNKS - 1
            total = [a[edge:edge + 1, :] for a in (ere, eim, are, aim)]
            enter = [shifted(ere, 1, 0.0), shifted(eim, 1, 0.0), shifted(are, 1, 1.0), shifted(aim, 1, 0.0)]
            return enter, total

        def send_carry(l, way, q, enter, total):
            msg, buf = v.ca_msg[l][way][q], v.ca_buf[l][way][q]
            msg[0:1, 0:SN] = total[0]
            msg[0:1, SN:] = total[1]
            msg[1:2, 0:SN] = total[2]
            msg[1:2, SN:] = total[3]
            v.cin[l][q, 0, :, 0:SN] = enter[0]
            v.cin[l][q, 0, :, SN:] = enter[1]
            v.cin[l][q, 1, :, 0:SN] = enter[2]
            v.cin[l][q, 1, :, SN:] = enter[3]
            buf[me_t] = msg[...]
            return send(STATE, msg, buf)

        def take_carry(l, way, q, got, reverse):
            got()
            buf = v.ca_buf[l][way][q]
            cre, cim = jnp.zeros((1, SN), F32), jnp.zeros((1, SN), F32)
            for j in (range(NT - 1, -1, -1) if reverse else range(NT)):
                before = (j > me_t) if reverse else (j < me_t)
                ere, eim = buf[j, 0:1, 0:SN], buf[j, 0:1, SN:]
                are, aim = buf[j, 1:2, 0:SN], buf[j, 1:2, SN:]
                nre, nim = are * cre - aim * cim + ere, are * cim + aim * cre + eim
                cre, cim = jnp.where(before, nre, cre), jnp.where(before, nim, cim)
            cin = v.cin[l]
            ere, eim = cin[q, 0, :, 0:SN], cin[q, 0, :, SN:]
            are, aim = cin[q, 1, :, 0:SN], cin[q, 1, :, SN:]
            return ere + are * cre - aim * cim, eim + are * cim + aim * cre

        def forward_step(l, q, nv, s, c):
            lre, lim, scale = lam(l)
            here = at_step(q, s)
            bre = v.proj[l][here, 0:SN] * scale
            bim = v.proj[l][here, SN:] * scale
            keep = s < nv
            cre, cim = c
            nre, nim = lre * cre - lim * cim + bre, lre * cim + lim * cre + bim
            return jnp.where(keep, nre, cre), jnp.where(keep, nim, cim)

        def scan_ends(l, q):
            reverse = l % 2 == 1
            nv = valid_count(q)
            zero = jnp.zeros((CHUNKS, SN), F32)
            ere, eim = steps(lambda s, c: forward_step(l, q, nv, s, c), (zero, zero), reverse)
            enter, total = chunk_scan(q, l, ere, eim, False, reverse)
            return send_carry(l, 0, q, enter, total)

        def scan_states(l, q, got):
            reverse = l % 2 == 1
            nv = valid_count(q)
            init = take_carry(l, 0, q, got, reverse)
            state, low = v.state[l], v.slow[l]
            edge = ST if reverse else 0
            state[q, edge * CHUNKS:(edge + 1) * CHUNKS, 0:SN] = init[0]
            state[q, edge * CHUNKS:(edge + 1) * CHUNKS, SN:] = init[1]

            def body(s, c):
                nre, nim = forward_step(l, q, nv, s, c)
                at = pl.ds(pl.multiple_of((s if reverse else s + 1) * CHUNKS, CHUNKS), CHUNKS)
                state[q, at, 0:SN] = nre
                state[q, at, SN:] = nim
                here = at_step(q, s)
                low[here, 0:SN] = nre.astype(BF16)
                low[here, SN:] = nim.astype(BF16)
                return nre, nim

            steps(body, init, reverse)

        def adjoint_step(l, q, nv, s, c):
            lre, lim, _ = lam(l)
            here = at_step(q, s)
            are = v.sgrad[here, 0:SN] + c[0]
            aim = v.sgrad[here, SN:] + c[1]
            keep = s < nv
            nre, nim = lre * are + lim * aim, lre * aim - lim * are
            return (are, aim), keep, (jnp.where(keep, nre, are), jnp.where(keep, nim, aim))

        def adjoint_ends(l, q):
            reverse = l % 2 == 0
            nv = valid_count(q)
            zero = jnp.zeros((CHUNKS, SN), F32)
            ere, eim = steps(lambda s, c: adjoint_step(l, q, nv, s, c)[2], (zero, zero), reverse)
            enter, total = chunk_scan(q, l, ere, eim, True, reverse)
            return send_carry(l, 1, q, enter, total)

        def adjoint_states(l, q, got, sums):
            reverse = l % 2 == 0
            nv = valid_count(q)
            init = take_carry(l, 1, q, got, reverse)
            state, proj = v.state[l], v.proj[l]
            _, _, scale = lam(l)

            def body(s, c):
                w, (gre, gim, gsc) = c
                (are, aim), keep, w = adjoint_step(l, q, nv, s, w)
                are, aim = jnp.where(keep, are, 0.0), jnp.where(keep, aim, 0.0)
                here = at_step(q, s)
                v.mlow[here, 0:SN] = (are * scale).astype(BF16)
                v.mlow[here, SN:] = (aim * scale).astype(BF16)
                at = pl.ds(pl.multiple_of((s if reverse else s + 1) * CHUNKS, CHUNKS), CHUNKS)
                pre, pim = state[q, at, 0:SN], state[q, at, SN:]
                gre = gre + are * pre + aim * pim
                gim = gim + aim * pre - are * pim
                gsc = gsc + are * proj[here, 0:SN] + aim * proj[here, SN:]
                return w, (gre, gim, gsc)

            return steps(body, (init, sums), reverse)[1]

        class Reduce:
            def __init__(self, refs, rr, cc, whole, turned):
                self.own, self.s, self.r, self.res = refs
                self.whole = whole
                self.axes = [CORE, Y, X, Z] if turned else [CORE, X, Y, Z]
                self.size = [rr // 2]
                for n, _, _ in self.axes[1:]:
                    self.size.append(self.size[-1] // n)
                self.split = self.size[3] % 16 == 0
                self.base = [0]
                for (_, coord, _), size in zip(self.axes[1:], self.size[1:]):
                    self.base.append(self.base[-1] + coord * size)
                self.stage = 0
                self.last = 8 if whole else 6
                self.got, self.sent = None, None

            def start(self):
                r = self.r[0]
                self.got, self.sent = exchange(CORE, lambda p, k: self.s, lambda c, k: r.at[0], lambda n: r)

            def rows(self, ref, start, count):
                return ref.at[pl.ds(pl.multiple_of(start, 8), count), :]

            def come(self, level, start, count):
                total = self.rows(self.own, self.base[level] + start, count)[...]
                n = self.axes[level][0]
                for k in range(n - 1):
                    total = total + self.r[level][k, pl.ds(pl.multiple_of(start, 8), count), :].astype(F32)
                return total

            def scatter(self, level):
                n, coord, _ = self.axes[level]
                size, r = self.size[level], self.r[level]
                self.sent()
                for k in range(n):
                    p = lax.rem(coord + k, n)
                    total = self.come(level - 1, p * size, size)
                    if k == 0:
                        self.rows(self.own, self.base[level - 1] + p * size, size)[...] = total
                    else:
                        self.rows(self.s, (k - 1) * size, size)[...] = total.astype(BF16)
                self.got, self.sent = exchange(
                    self.axes[level], lambda p, k: self.rows(self.s, (k - 1) * size, size),
                    lambda c, k: r.at[k - 1], lambda m: r)

            def place(self, level):
                if self.whole:
                    at = core * self.size[0] + self.base[level]
                else:
                    at = my * self.size[2] + (self.base[3] - self.base[2] if level == 3 else 0)
                return self.rows(self.res, at, self.size[level])

            def gather(self, level):
                spot, r = self.place(level), self.r[level]
                self.got, self.sent = exchange(
                    self.axes[level], lambda p, k: spot, lambda c, k: spot, lambda m: r)

            def step(self):
                k = self.stage
                self.stage += 1
                if self.got is not None:
                    self.got()
                    self.got = None
                if k < 2 or (k == 2 and self.split):
                    self.scatter(k + 1)
                elif k == 2:
                    size, r = self.size[2], self.r[3]
                    self.sent()
                    spot = self.rows(self.s, 0, size)
                    spot[...] = self.come(2, 0, size).astype(BF16)
                    r[mz] = spot[...]
                    self.got, self.sent = exchange(
                        Z, lambda p, j: spot, lambda c, j: r.at[c], lambda m: r.at[pl.ds(0, m)])
                elif k == 3 and self.split:
                    self.place(3)[...] = self.come(3, 0, self.size[3]).astype(BF16)
                    self.gather(3)
                elif k == 3:
                    self.place(2)[...] = jnp.sum(self.r[3][...].astype(F32), axis=0).astype(BF16)
                elif k == 4:
                    if self.whole or self.axes[2] is Y:
                        self.gather(2)
                    else:
                        spot = self.place(2)
                        self.got, self.sent = exchange(
                            Y, lambda p, j: spot, lambda c, j: spot, lambda m: self.rows(self.res, 0, m * self.size[2]))
                elif k == 5 and self.whole:
                    self.gather(1)
                elif k == 6 and self.whole:
                    self.gather(0)

        reducers = [
            [[Reduce(v.red[l][k][half], *kinds[k], half == 1) for half in range(2)] for k in range(3)] for l in range(2)
        ]

        def glu_gradient(l):
            h, w = D // 2, E // 2
            for which in (0, 1):
                at = pl.ds(pl.multiple_of((core if which else 1 - core) * h, 128), h)
                for half, red in enumerate(reducers[l][0]):
                    part = dot_tn(v.hid[l][:, at], v.bothg[:, half * w:(half + 1) * w])
                    if which:
                        red.own[...] = part
                    else:
                        red.s[...] = part.astype(BF16)
                        red.start()

        def state_matrix_gradient(pair, left, right):
            p = 2 * NL // NY
            unit = min(p, NL)
            for c in range(2):
                v.full[...] = dot_tn(left[:, c * SN:(c + 1) * SN], right[...])
                for half, red in enumerate(pair):
                    cols = slice(half * (D // 2), (half + 1) * (D // 2))
                    for x in range(NX):
                        for part in range(NL // unit):
                            j = c * NL + part * unit
                            dst = ((j // p) * NX + x) * p + j % p if half else x * 2 * NL + j
                            mine = pl.ds(pl.multiple_of((x * 2 + core) * NL + part * unit, 8), unit)
                            theirs = pl.ds(pl.multiple_of((x * 2 + 1 - core) * NL + part * unit, 8), unit)
                            red.s[dst:dst + unit, :] = v.full[theirs, cols].astype(BF16)
                            red.own[dst:dst + unit, :] = v.full[mine, cols]
            for red in pair:
                red.start()

        def take_flat(dst):
            v.flat[...] = v.raw[...].astype(F32)

            def body(s, c):
                for q in range(Q):
                    for j in range(LT):
                        part = v.flat[pl.ds(s * (LT * Q) + j * Q + q, CHUNKS, stride=ST * LT * Q), :]
                        dst[at_step(q, s), j * 128:(j + 1) * 128] = part.astype(BF16)
                return c

            lax.fori_loop(0, ST, body, 0)

        def put_flat(r, q, tile):
            for i in range(RT // CHUNKS):
                for j in range(LT):
                    v.flat[pl.ds((r // CHUNKS + i) * (LT * Q) + j * Q + q, CHUNKS, stride=ST * LT * Q), :] = (
                        tile[i * CHUNKS:(i + 1) * CHUNKS, j * 128:(j + 1) * 128])

        def weight(ref):
            return ref[...].reshape(SL2, D)

        def forward_tile(l, r):
            at = pl.ds(r, RT)
            u = read_u(l)(r)
            _, normed = normalise(l, u)
            mixed = dot_nn(v.slow[l][at, :], weight(v.wout[l]))
            x = mixed + skip_ref[l:l + 1, :] * normed
            x2 = x * x
            t = jnp.tanh(x * (GELU_A + (GELU_A * GELU_B) * x2))
            half = 0.5 * (1.0 + t)
            hidden = (x * half).astype(BF16)
            v.hid[l][at, :] = hidden
            dgelu = half + (0.5 * x) * (1.0 - t * t) * (GELU_A + (3.0 * GELU_A * GELU_B) * x2)
            both = dot_nn(hidden, v.wglu[l])
            linear = both[:, :D]
            gate = 0.5 + 0.5 * jnp.tanh(0.5 * both[:, D:])
            return u, normed, dgelu, linear, gate

        def backward_tile(l, r, upstream, normed, dgelu, linear, gate):
            at = pl.ds(r, RT)
            pass_gate = upstream * gate
            bothg = jnp.concatenate([pass_gate, pass_gate * linear * (1.0 - gate)], axis=1).astype(BF16)
            v.bothg[at, :] = bothg
            preg = dot_nt(bothg, v.wglu[l]) * dgelu
            v.preg[at, :] = preg
            mlow = preg.astype(BF16)
            v.mlow[at, :] = mlow
            v.sgrad[at, :] = dot_nt(mlow, weight(v.wout[l]))
            return fold8(preg * normed)

        def norm_grads(l, q, sums):
            def body(r, c):
                at = pl.ds(r + q * L, RT)
                standard, _ = normalise(l, read_u(l)(r + q * L))
                ng = v.preg[at, :] * skip_ref[l:l + 1, :] + dot_nn(v.mlow[at, :], weight(v.win[l]))
                v.preg[at, :] = ng
                return c[0] + fold8(ng), c[1] + fold8(ng * standard)
            return tiles(body, sums, TILES)

        def send_norm_grads(l, sums):
            msg, buf = v.bw_msg[l], v.bw_buf[l]
            msg[0:1, :] = fold1(sums[0])
            msg[1:2, :] = fold1(sums[1])
            buf[me] = msg[...]
            return send(ALL, msg, buf)

        def put_small(l, skip, chain):
            msg, r = v.sm_msg, 4 * l
            msg[r:r + 1, :] = fold1(skip)
            msg[r + 1:r + 2, 0:SN] = fold1(chain[0])
            msg[r + 1:r + 2, SN:] = fold1(chain[1])
            msg[r + 2:r + 3, 0:SN] = fold1(chain[2])
            msg[r + 2:r + 3, SN:] = jnp.zeros((1, SN), F32)
            msg[r + 3:r + 4, :] = jnp.zeros((1, D), F32)

        def send_small():
            v.sm_buf[me_t] = v.sm_msg[...]
            return send(STATE, v.sm_msg, v.sm_buf)

        def pass_small(got):
            got()
            v.sm_sum[...] = jnp.sum(v.sm_buf[...], axis=0)
            v.sm_all[me_s] = v.sm_sum[...]
            return send(SEQ, v.sm_sum, v.sm_all)

        def take_norm_grads(l, got):
            got()
            buf = v.bw_buf[l]
            total = jnp.sum(buf[...], axis=0)
            v.small[l][0:2, :] = total

        def take_small(got):
            got()
            total = jnp.sum(v.sm_all[...], axis=0)
            out = v.result
            out[...] = jnp.zeros((16, D), F32)

            def mine(row):
                held = jnp.zeros((1, NL), F32)
                for j in range(NT):
                    held = jnp.where(me_t == j, row[:, j * NL:(j + 1) * NL], held)
                return held

            for l in range(2):
                out[l:l + 1, :] = v.small[l][1:2, :]
                out[2 + l:3 + l, :] = v.small[l][0:1, :]
                out[4 + l:5 + l, :] = total[4 * l:4 * l + 1, :]
                sum_re = mine(total[4 * l + 1:4 * l + 2, 0:SN])
                sum_im = mine(total[4 * l + 1:4 * l + 2, SN:])
                sum_sc = mine(total[4 * l + 2:4 * l + 3, 0:SN])
                own = slice(l, l + 1)
                rate = jnp.exp(nu_ref[own, :])
                phase = jnp.exp(theta_ref[own, :])
                lre, lim = v.par_msg[3 * l:3 * l + 1, 0:NL], v.par_msg[3 * l + 1:3 * l + 2, 0:NL]
                slow = jnp.tanh(rate)
                root = jnp.sqrt(2.0 * slow / (1.0 + slow))
                rate_grad = sum_sc * gamma_ref[own, :] * jnp.exp(-2.0 * rate) / root - (sum_re * lre + sum_im * lim)
                out[6 + l:7 + l, 0:NL] = rate * rate_grad
                out[8 + l:9 + l, 0:NL] = phase * (sum_im * lre - sum_re * lim)
                out[10 + l:11 + l, 0:NL] = sum_sc * root

        def input_gradient(l, r, upstream):
            stat, small = v.stat[l], v.small[l]
            standard, _ = normalise(l, read_u(l)(r))
            m = rep(v.mask[pl.ds(r, RT), :])
            inner = small[0:1, :] + standard * small[1:2, :]
            ng = v.preg[pl.ds(r, RT), :] - m * inner / stat[2:3, :]
            return upstream + stat[1:2, :] * gain_ref[l:l + 1, :] * ng

        rate = jnp.exp(nu_ref[...])
        phase = jnp.exp(theta_ref[...])
        modulus = jnp.exp(-rate)
        lam_re, lam_im = modulus * jnp.cos(phase), modulus * jnp.sin(phase)
        slow = jnp.tanh(rate)
        root = jnp.sqrt(2.0 * slow / (1.0 + slow))
        scale_own = gamma_ref[...] * root
        v.par_msg[...] = jnp.zeros((8, 128), F32)
        v.len_msg[...] = jnp.zeros((8, 128), F32)
        for l in range(2):
            for i, row in enumerate((lam_re, lam_im, scale_own)):
                v.par_msg[3 * l + i:3 * l + i + 1, 0:NL] = row[l:l + 1, :]
        v.par_buf[me_t] = v.par_msg[...]
        for q in range(Q):
            v.len_msg[q:q + 1, :] = jnp.full((1, 128), 1.0, F32) * len_ref[q].astype(F32)
        v.len_buf[me_s] = v.len_msg[...]

        base = me_t * L
        row = lax.broadcasted_iota(jnp.int32, (L, 128), 0)
        token = base + lax.rem(row, CHUNKS) * ST + row // CHUNKS
        count_own = jnp.float32(0)
        for q in range(Q):
            v.mask[q * L:(q + 1) * L, :] = (token < len_ref[q]).astype(F32)
            count_own = count_own + jnp.clip(len_ref[q] - base, 0, L).astype(F32)

        got_x()
        take_flat(v.x0)
        got_cot = load(cot_hbm, v.raw)
        local_stats(read_u(0), 0)
        for wait in got_own:
            wait()
        pl.semaphore_wait(barrier, N - 1)
        got_len = send(SEQ, v.len_msg, v.len_buf)
        got = send(ALL, v.st_msg[0], v.st_buf[0])
        got_par = send(STATE, v.par_msg, v.par_buf)
        gathers = [[Gather(v.win[0]), Gather(v.wout[0])], []]
        got_par()
        v.par[...] = jnp.concatenate([v.par_buf[j, :, 0:NL] for j in range(NT)], axis=1)
        chunk_powers(0)
        chunk_powers(1)
        take_counts()
        gathers[0][0].relay()
        global_stats(0, got)
        gathers[0][1].relay()

        def project(l, q):
            def body(r, c):
                at = pl.ds(r + q * L, RT)
                _, normed = normalise(l, read_u(l)(r + q * L))
                low = normed.astype(BF16)
                v.nlow[l][at, :] = low
                v.proj[l][at, :] = dot_nt(low, weight(v.win[l]))
                return c
            tiles(body, 0, TILES)

        def forward_scan(l, between):
            gathers[l][0].take()
            waits = []
            for q in range(Q):
                project(l, q)
                waits.append(scan_ends(l, q))
            gathers[l][1].take()
            v.wout[l][1] = -v.wout[l][1]
            between()
            return waits

        def more_weights():
            gathers[1].append(Gather(v.win[1]))
            gathers[1].append(Gather(v.wout[1]))

        waits = forward_scan(0, more_weights)
        got_glu()
        total = zero8
        for q in range(Q):
            scan_states(0, q, waits[q])

            def body(r, acc, q=q):
                at = pl.ds(r + q * L, RT)
                u, normed, dgelu, linear, gate = forward_tile(0, r + q * L)
                v.dgelu[at, :] = dgelu
                v.lin[at, :] = linear
                v.gate[at, :] = gate
                u = u + linear * gate
                v.u1[at, :] = u
                return acc + fold8(u * rep(v.mask[at, :]))

            total = tiles(body, total, TILES)
            gathers[1][q % 2].relay()

        local_stats(read_u(1), 1, total)
        got = send(ALL, v.st_msg[1], v.st_buf[1])
        got_cot()
        take_flat(v.cot)
        global_stats(1, got)
        waits = forward_scan(1, lambda: None)
        skip = zero8
        waits_b = []
        for q in range(Q):
            scan_states(1, q, waits[q])

            def body(r, acc, q=q):
                at = pl.ds(r + q * L, RT)
                u, normed, dgelu, linear, gate = forward_tile(1, r + q * L)
                v.up[at, :] = u + linear * gate
                upstream = v.cot[at, :].astype(F32)
                return acc + backward_tile(1, r + q * L, upstream, normed, dgelu, linear, gate)

            skip = tiles(body, skip, TILES)
            waits_b.append(adjoint_ends(1, q))

        def advance(*which):
            for pair in which:
                for red in pair:
                    if red.stage < red.last:
                        red.step()

        def finish_backward(l, waits_b, skip, after_mixer, after_sends):
            g, o, i = reducers[l]
            glu_gradient(l)
            state_matrix_gradient(o, v.slow[l], v.mlow)
            advance(g)
            chain = (jnp.zeros((CHUNKS, SN), F32),) * 3
            sums = (zero8, zero8)
            for q in range(Q):
                chain = adjoint_states(l, q, waits_b[q], chain)
                if l == 1:
                    sums = norm_grads(l, q, sums)
            put_small(l, skip, chain)
            if l == 0:
                state_matrix_gradient(i, v.mlow, v.nlow[l])
                after_mixer()
                for q in range(Q):
                    sums = norm_grads(l, q, sums)
            got = send_norm_grads(l, sums)
            if l == 1:
                state_matrix_gradient(i, v.mlow, v.nlow[l])
            after_sends()
            take_norm_grads(l, got)

        (g0, o0, i0), (g1, o1, i1) = reducers
        stored = []

        def give_u2():
            advance(o1)
            for q in range(Q):
                def body(r, c, q=q):
                    put_flat(r, q, v.up[pl.ds(r + q * L, RT), :])
                    return c
                tiles(body, 0, TILES)
            stored.append(load(v.flat, u2_out))
            advance(i1, g1)

        finish_backward(1, waits_b, skip, None, give_u2)

        skip = zero8
        waits_b = []
        for q in range(Q):
            def body(r, acc, q=q):
                at = pl.ds(r + q * L, RT)
                upstream = input_gradient(1, r + q * L, v.cot[at, :].astype(F32))
                v.up[at, :] = upstream
                _, normed = normalise(0, read_u(0)(r + q * L))
                return acc + backward_tile(0, r + q * L, upstream, normed, v.dgelu[at, :], v.lin[at, :], v.gate[at, :])

            skip = tiles(body, skip, TILES)
            waits_b.append(adjoint_ends(0, q))
            if q == 0:
                advance(o1, i1)
            else:
                advance(g1)

        got_small = []

        def after_mixer():
            got_small.append(send_small())
            advance(o0)

        def after_sends():
            advance(i0, g0, o0, o1, i1, g1)

        finish_backward(0, waits_b, skip, after_mixer, after_sends)
        advance(g0, i0)
        got_small = pass_small(got_small[0])
        stored[0]()

        for q in range(Q):
            def body(r, c, q=q):
                put_flat(r, q, input_gradient(0, r + q * L, v.up[pl.ds(r + q * L, RT), :]))
                return c

            tiles(body, 0, TILES)
        stored = [load(v.flat, ig_out)]
        take_small(got_small)
        stored.append(load(v.result, small_out))
        order = [g0, i0, o0, g1, o1, i1]
        while any(pair[0].stage < pair[0].last for pair in order):
            for pair in order:
                advance(pair)
        for l in range(2):
            for half in range(2):
                stored.append(load(reducers[l][0][half].res, glu_out.at[l, half]))
                stored.append(load(reducers[l][1][half].res, out_out.at[l, half]))
                stored.append(load(reducers[l][2][half].res, int_out.at[l, half]))
        for w in pending:
            w()

    out_shape = [
        jax.ShapeDtypeStruct((FLAT, 128), F32),
        jax.ShapeDtypeStruct((FLAT, 128), F32),
        jax.ShapeDtypeStruct((16, D), F32),
        jax.ShapeDtypeStruct((2, 2, 2 * NL, D // 2), BF16),
        jax.ShapeDtypeStruct((2, 2, 2 * NL, D // 2), BF16),
        jax.ShapeDtypeStruct((2, 2, D, E // 2), BF16),
    ]
    hbm = pl.BlockSpec(memory_space=pl.ANY)
    vmem = pl.BlockSpec(memory_space=pltpu.VMEM)
    smem = pl.BlockSpec(memory_space=pltpu.SMEM)
    return pl.pallas_call(
        kernel,
        out_shape=out_shape,
        in_specs=[hbm, hbm, smem] + [vmem] * 6 + [hbm] * 3,
        out_specs=[hbm] * 6,
        scratch_shapes=scratch,
        compiler_params=pltpu.CompilerParams(
            collective_id=0, has_side_effects=True, vmem_limit_bytes=VMEM_LIMIT
        ),
    )


def finish(rows, seqs, width, own):
    D, NL = width, own
    FLAT = rows * seqs * D // 128

    def kernel(u2, ig, small, ing, outg, glu, u2_o, ig_o, gain_o, bias_o, skip_o, nu_o, theta_o, gamma_o, in_o, out_o, glu_o,
               wide, glu_low, glu_wide, in_low, out_low, in_wide, out_wide, sems):
        count = []

        def copy(src, dst):
            c = pltpu.make_async_copy(src, dst, sems.at[len(count)])
            count.append(c)
            c.start()
            return c

        got_glu = [copy(glu.at[l], glu_low.at[l]) for l in range(2)]
        got_u2, got_ig = copy(u2, wide.at[0]), copy(ig, wide.at[1])
        got_in, got_out = copy(ing, in_low), copy(outg, out_low)
        back = []
        for l in range(2):
            got_glu[l].wait()
            for half in range(2):
                glu_wide[l, :, half * D:(half + 1) * D] = glu_low[l, half].astype(F32)
            back.append(copy(glu_wide.at[l], glu_o.at[l]))
        got_u2.wait()
        back.append(copy(wide.at[0], u2_o))
        got_ig.wait()
        back.append(copy(wide.at[1], ig_o))
        got_in.wait()
        got_out.wait()
        for l in range(2):
            for half in range(2):
                cols = slice(half * (D // 2), (half + 1) * (D // 2))
                for c in range(2):
                    part = out_low[l, half, c * NL:(c + 1) * NL, :].astype(F32)
                    out_wide[l, c, :, cols] = -part if c else part
                    in_wide[l, c, :, cols] = in_low[l, half, c * NL:(c + 1) * NL, :].astype(F32)
        back += [copy(in_wide, in_o), copy(out_wide, out_o)]
        for l in range(2):
            for ref, at in ((gain_o, 0), (bias_o, 2), (skip_o, 4)):
                ref[l:l + 1, :] = small[at + l:at + l + 1, :]
            for ref, at in ((nu_o, 6), (theta_o, 8), (gamma_o, 10)):
                ref[l:l + 1, :] = small[at + l:at + l + 1, 0:NL]
        for b in back:
            b.wait()

    f32 = lambda *shape: jax.ShapeDtypeStruct(shape, F32)
    hbm = pl.BlockSpec(memory_space=pl.ANY)
    vmem = pl.BlockSpec(memory_space=pltpu.VMEM)
    return pl.pallas_call(
        kernel,
        out_shape=[f32(FLAT, 128), f32(FLAT, 128)] + [f32(2, D)] * 3 + [f32(2, NL)] * 3
        + [f32(2, 2, NL, D), f32(2, 2, NL, D), f32(2, D, 2 * D)],
        in_specs=[hbm, hbm, vmem] + [hbm] * 3,
        out_specs=[hbm, hbm] + [vmem] * 6 + [hbm] * 3,
        scratch_shapes=[
            pltpu.VMEM((2, FLAT, 128), F32),
            pltpu.VMEM((2, 2, D, D), BF16),
            pltpu.VMEM((2, D, 2 * D), F32),
            pltpu.VMEM((2, 2, 2 * NL, D // 2), BF16),
            pltpu.VMEM((2, 2, 2 * NL, D // 2), BF16),
            pltpu.VMEM((2, 2, NL, D), F32),
            pltpu.VMEM((2, 2, NL, D), F32),
            pltpu.SemaphoreType.DMA((12,)),
        ],
        compiler_params=pltpu.CompilerParams(vmem_limit_bytes=VMEM_LIMIT),
    )


def solution(mesh):
    seq_devices, state_devices = mesh.shape["seq"], mesh.shape["state"]

    def per_device(
        inputs, lengths, norm_gain, norm_bias, in_proj, out_proj,
        nu_log, theta_log, gamma_gain, skip_gain, glu_weight, cotangent,
    ):
        rows, seqs, width = inputs.shape
        layers, own = nu_log.shape
        lanes = width // 128

        def flat(a):
            a = a.reshape(rows, seqs, lanes, 128).transpose(0, 2, 1, 3)
            return a.reshape(rows * seqs * lanes, 128)

        def by_tokens(a):
            a = a.reshape(rows, lanes, seqs, 128).transpose(0, 2, 1, 3)
            return a.reshape(rows, seqs, width)

        step = build(seq_devices, state_devices, rows, seqs, width, own, layers)
        held = step(
            flat(inputs), flat(cotangent), lengths, norm_gain, norm_bias, nu_log, theta_log, gamma_gain, skip_gain,
            jnp.swapaxes(in_proj, 2, 3), out_proj, glu_weight,
        )
        u2, input_grad, gain, bias, skip, nu, theta, gamma, in_grad, out_grad, glu = finish(rows, seqs, width, own)(*held)
        return by_tokens(u2), by_tokens(input_grad), gain, bias, jnp.swapaxes(in_grad, 2, 3), out_grad, nu, theta, gamma, skip, glu

    return jax.shard_map(
        per_device,
        mesh=mesh,
        in_specs=(
            P("state", "seq", None),
            P("seq"),
            P(),
            P(),
            P(None, None, None, "state"),
            P(None, None, "state", None),
            P(None, "state"),
            P(None, "state"),
            P(None, "state"),
            P(),
            P(),
            P("state", "seq", None),
        ),
        out_specs=(
            P("state", "seq", None),
            P("state", "seq", None),
            P(),
            P(),
            P(None, None, None, "state"),
            P(None, None, "state", None),
            P(None, "state"),
            P(None, "state"),
            P(None, "state"),
            P(),
            P(),
        ),
        check_vma=False,
    )
```

```python
import math

import jax
import jax.numpy as jnp
from jax import lax
from jax.experimental import pallas as pl
from jax.experimental.pallas import tpu as pltpu
from jax.sharding import PartitionSpec as P

EPSILON = 1e-05
MESH = pl.DeviceIdType.MESH
F32 = jnp.float32
BF16 = jnp.bfloat16
CHUNKS = 16
GELU_A = math.sqrt(2.0 / math.pi)
GELU_B = 0.044715
VMEM_LIMIT = 65280 * 1024


def dot_nn(a, b):
    return lax.dot_general(a, b, (((1,), (0,)), ((), ())), preferred_element_type=F32)


def dot_nt(a, b):
    return lax.dot_general(a, b, (((1,), (1,)), ((), ())), preferred_element_type=F32)


def dot_tn(a, b):
    return lax.dot_general(a, b, (((0,), (0,)), ((), ())), preferred_element_type=F32)


class Buffers:
    def __init__(self):
        self.shapes = []

    def add(self, shape, dtype):
        self.shapes.append(pltpu.VMEM(shape, dtype))
        return len(self.shapes) - 1

    def bind(self, refs):
        bound = Buffers()
        for key, places in vars(self).items():
            if places is not self.shapes:
                setattr(bound, key, jax.tree.map(lambda i: refs[i], places))
        return bound


def build(axis_seq, axis_state, rows, seqs, width, states_own, layers):
    NS, NT = axis_seq, axis_state
    N = NS * NT
    NX = NT // 2
    NY = NX if NS % NX == 0 else 1
    NZ = NS // NY
    L, Q, D, NL = rows, seqs, width, states_own
    ST = L // CHUNKS
    SN = NL * NT
    SL2 = 2 * SN
    E = 2 * D
    T = Q * L
    RT = min(512, L)
    TILES = L // RT
    UN = 4
    assert layers == 2 and NT % 2 == 0 and L % CHUNKS == 0

    v = Buffers()
    vm = v.add
    LT = D // 128
    FLAT = T * LT
    v.raw = vm((FLAT, 128), BF16)
    v.flat = vm((FLAT, 128), F32)
    v.x0 = vm((T, D), BF16)
    v.cot = vm((T, D), BF16)
    v.u1 = vm((T, D), F32)
    v.mask = vm((T, 128), F32)
    v.nlow, v.slow, v.hid = ([vm((T, D), BF16) for _ in range(2)] for _ in range(3))
    v.proj = [vm((T, SL2), F32) for _ in range(2)]
    v.state = [vm((Q, (ST + 1) * CHUNKS, SL2), F32) for _ in range(2)]
    v.apow = [vm((Q, 2, CHUNKS, SN), F32) for _ in range(2)]
    v.cin = [vm((Q, 2, CHUNKS, SL2), F32) for _ in range(2)]
    v.win, v.wout = ([vm((2, NT, NL, D), BF16) for _ in range(2)] for _ in range(2))
    v.st_msg, v.bw_msg = ([vm((2, D), F32) for _ in range(2)] for _ in range(2))
    v.st_buf, v.bw_buf = ([vm((N, 2, D), F32) for _ in range(2)] for _ in range(2))
    v.len_msg = vm((8, 128), F32)
    v.len_buf = vm((NS, 8, 128), F32)
    v.sm_msg = vm((8, D), F32)
    v.sm_buf = vm((NT, 8, D), F32)
    v.sm_sum = vm((8, D), F32)
    v.sm_all = vm((NS, 8, D), F32)
    v.stat, v.small = ([vm((8, D), F32) for _ in range(2)] for _ in range(2))
    v.ca_msg = [[[vm((2, SL2), F32) for _ in range(Q)] for _ in range(2)] for _ in range(2)]
    v.ca_buf = [[[vm((NT, 2, SL2), F32) for _ in range(Q)] for _ in range(2)] for _ in range(2)]
    v.dgelu, v.lin, v.gate, v.preg, v.up = (vm((T, D), F32) for _ in range(5))
    v.wglu = vm((2, D, E), BF16)
    v.bothg = vm((T, E), BF16)
    v.mlow = vm((T, D), BF16)
    v.sgrad = vm((T, SL2), F32)
    v.par_msg = vm((8, 128), F32)
    v.par_buf = vm((NT, 8, 128), F32)
    v.par = vm((8, SN), F32)
    v.result = vm((16, D), F32)
    v.counts = vm((N, 1, D), F32)
    v.full = vm((SN, D), F32)

    def reduce_buffers(rr, cc, whole, turned):
        h = rr // 2
        n1, n2 = (NY, NX) if turned else (NX, NY)
        p1 = h // n1
        p2 = p1 // n2
        p3 = p2 // NZ
        last = (NZ - 1, p3, cc) if p3 % 16 == 0 else (NZ, p2, cc)
        return [
            vm((h, cc), F32),
            vm((h, cc), BF16),
            [vm((1, h, cc), BF16), vm((max(n1 - 1, 1), p1, cc), BF16), vm((max(n2 - 1, 1), p2, cc), BF16), vm(last, BF16)],
            vm((rr if whole else 2 * NL, cc), BF16),
        ]

    kinds = [(D, E // 2, True), (SL2, D // 2, False), (SL2, D // 2, False)]
    v.red = [[[reduce_buffers(*kind, turned) for turned in (False, True)] for kind in kinds] for _ in range(2)]
    places = v
    SEMS = 160
    scratch = v.shapes + [
        pltpu.SemaphoreType.DMA((SEMS,)),
        pltpu.SemaphoreType.DMA((SEMS,)),
        pltpu.SemaphoreType.DMA((SEMS,)),
    ]

    def kernel(
        x_hbm, cot_hbm, len_ref, gain_ref, bias_ref, nu_ref, theta_ref, gamma_ref, skip_ref, win_hbm, wout_hbm, glu_hbm,
        u2_out, ig_out, small_out, int_out, out_out, glu_out, *rest,
    ):
        v = places.bind(rest[: len(places.shapes)])
        ssem, rsem, lsem = rest[len(places.shapes):]
        me_s, me_t = lax.axis_index("seq"), lax.axis_index("state")
        me = me_s * NT + me_t
        core, mx = lax.rem(me_t, 2), me_t // 2
        my, mz = lax.rem(me_s, NY), me_s // NY
        CORE = (2, core, lambda p: (me_s, mx * 2 + p))
        X = (NX, mx, lambda p: (me_s, p * 2 + core))
        Y = (NY, my, lambda p: (mz * NY + p, me_t))
        Z = (NZ, mz, lambda p: (p * NY + my, me_t))
        STATE = (NT, me_t, lambda p: (me_s, p))
        SEQ = (NS, me_s, lambda p: (p, me_t))
        ALL = (N, me, lambda p: (p // NT, lax.rem(p, NT)))
        remotes, locals_, pending = [], [], []

        def once(wait):
            left = [wait]
            pending.append(lambda: left.pop()() if left else None)
            return pending[-1]

        def wait_bytes(view, sem):
            pltpu.make_async_copy(view, view, sem).wait()

        def exchange(axis, src_of, dst_of, size_view):
            n, coord, dev = axis
            k = len(remotes)
            remotes.append(k)
            assert k < SEMS
            if n == 1:
                return once(lambda: None), once(lambda: None)

            def one(step):
                p = lax.rem(coord + step, n)
                pltpu.make_async_remote_copy(
                    src_ref=src_of(p, step), dst_ref=dst_of(coord, step), send_sem=ssem.at[k],
                    recv_sem=rsem.at[k], device_id=dev(p), device_id_type=MESH,
                ).start()

            if n <= 8:
                for step in range(1, n):
                    one(step)
            else:
                def body(step, c):
                    one(step)
                    return c
                lax.fori_loop(1, n, body, 0)
            return (
                once(lambda: wait_bytes(size_view(n - 1), rsem.at[k])),
                once(lambda: wait_bytes(size_view(n - 1), ssem.at[k])),
            )

        def send(axis, src, buf):
            return exchange(axis, lambda p, k: src, lambda c, k: buf.at[c], lambda n: buf.at[pl.ds(0, n)])[0]

        def load(src, dst):
            k = len(locals_)
            locals_.append(k)
            copy = pltpu.make_async_copy(src, dst, lsem.at[k])
            copy.start()
            return once(copy.wait)

        got_x = load(x_hbm, v.raw)
        got_own = [load(hbm.at[l], dst[l].at[:, me_t]) for l in range(2) for hbm, dst in ((win_hbm, v.win), (wout_hbm, v.wout))]
        got_glu = load(glu_hbm, v.wglu)

        barrier = pltpu.get_barrier_semaphore()

        def greet(step, c):
            p = lax.rem(me + step, N)
            pl.semaphore_signal(barrier, inc=1, device_id=(p // NT, lax.rem(p, NT)), device_id_type=MESH)
            return c

        lax.fori_loop(1, N, greet, 0)

        class Gather:
            def __init__(self, dst):
                self.dst = dst
                self.x = self.spread(X, me_t)
                self.rest = [self.spread(CORE, me_t)]

            def spread(self, axis, slot):
                spot = self.dst.at[:, slot]
                return exchange(axis, lambda p, k: spot, lambda c, k: spot, lambda n: self.dst.at[:, pl.ds(0, n)])

            def relay(self):
                self.x[0]()
                self.rest += [self.spread(CORE, lax.rem(mx + k, NX) * 2 + core) for k in range(1, NX)]

            def take(self):
                self.x[1]()
                for came, sent in self.rest:
                    came()
                    sent()

        def rep(m, w=D):
            return jnp.concatenate([m] * (w // 128), axis=1)

        def tiles(body, init, count=T // RT):
            return lax.fori_loop(0, count, lambda i, c: body(pl.multiple_of(i * RT, RT), c), init)

        def fold8(a):
            return jnp.sum(a.reshape(a.shape[0] // 8, 8, a.shape[1]), axis=0)

        def fold1(a):
            return jnp.sum(a, axis=0, keepdims=True)

        zero8 = jnp.zeros((8, D), F32)

        def local_stats(read, l, total=None):
            if total is None:
                def add(r, acc):
                    return acc + fold8(read(r) * rep(v.mask[pl.ds(r, RT), :]))
                total = tiles(add, zero8)
            mean_own = fold1(total) / jnp.maximum(count_own, 1.0)

            def spread(r, acc):
                c = read(r) - mean_own
                return acc + fold8(c * c * rep(v.mask[pl.ds(r, RT), :]))

            squares = fold1(tiles(spread, zero8))
            v.st_msg[l][0:1, :] = mean_own
            v.st_msg[l][1:2, :] = squares
            v.st_buf[l][me] = v.st_msg[l][...]

        def global_stats(l, got):
            got()
            buf = v.st_buf[l]
            means, squares = buf[:, 0:1, :], buf[:, 1:2, :]
            counts = v.counts[...]
            count = jnp.sum(counts, axis=0)
            mean = jnp.sum(means * counts, axis=0) / count
            off = means - mean[None]
            variance = jnp.sum(squares + counts * off * off, axis=0) / count
            stat = v.stat[l]
            stat[0:1, :] = mean
            stat[1:2, :] = lax.rsqrt(variance + EPSILON)
            stat[2:3, :] = count

        def take_counts():
            got_len()
            for s in range(NS):
                for t in range(NT):
                    held = jnp.zeros((1, 128), F32)
                    for q in range(Q):
                        held = held + jnp.clip(v.len_buf[s, q:q + 1, :] - float(t * L), 0.0, float(L))
                    v.counts[s * NT + t] = rep(held)

        def normalise(l, u):
            stat = v.stat[l]
            standard = (u - stat[0:1, :]) * stat[1:2, :]
            return standard, standard * gain_ref[l:l + 1, :] + bias_ref[l:l + 1, :]

        def read_u(l):
            if l == 0:
                return lambda r: v.x0[pl.ds(r, RT), :].astype(F32)
            return lambda r: v.u1[pl.ds(r, RT), :]

        def valid_count(q):
            chunk = lax.broadcasted_iota(jnp.int32, (CHUNKS, SN), 0)
            return jnp.clip(len_ref[q] - base - chunk * ST, 0, ST)

        def lam(l):
            return v.par[3 * l:3 * l + 1, :], v.par[3 * l + 1:3 * l + 2, :], v.par[3 * l + 2:3 * l + 3, :]

        def chunk_powers(l):
            for q in range(Q):
                nv = valid_count(q)
                lre, lim, _ = lam(l)
                lre = jnp.broadcast_to(lre, (CHUNKS, SN))
                lim = jnp.broadcast_to(lim, (CHUNKS, SN))
                pre, pim = jnp.ones((CHUNKS, SN), F32), jnp.zeros((CHUNKS, SN), F32)
                bit = 1
                while bit <= ST:
                    on = (nv & bit) != 0
                    nre, nim = pre * lre - pim * lim, pre * lim + pim * lre
                    pre, pim = jnp.where(on, nre, pre), jnp.where(on, nim, pim)
                    lre, lim = lre * lre - lim * lim, 2.0 * lre * lim
                    bit *= 2
                v.apow[l][q, 0] = pre
                v.apow[l][q, 1] = pim

        def steps(body, init, reverse):
            def outer(i, c):
                for j in range(UN):
                    s = i * UN + j
                    if reverse:
                        s = ST - 1 - s
                    c = body(s, c)
                return c
            return lax.fori_loop(0, ST // UN, outer, init)

        def at_step(q, s):
            return pl.ds(pl.multiple_of(q * L + s * CHUNKS, CHUNKS), CHUNKS)

        def chunk_scan(q, l, end_re, end_im, conj, reverse):
            are, aim = v.apow[l][q, 0], v.apow[l][q, 1]
            if conj:
                aim = -aim
            ere, eim = end_re, end_im
            chunk = lax.broadcasted_iota(jnp.int32, (CHUNKS, SN), 0)

            def shifted(a, d, fill):
                if reverse:
                    return jnp.where(chunk < CHUNKS - d, pltpu.roll(a, CHUNKS - d, 0), fill)
                return jnp.where(chunk >= d, pltpu.roll(a, d, 0), fill)

            d = 1
            while d < CHUNKS:
                sre, sim = shifted(ere, d, 0.0), shifted(eim, d, 0.0)
                tre, tim = shifted(are, d, 1.0), shifted(aim, d, 0.0)
                ere, eim = are * sre - aim * sim + ere, are * sim + aim * sre + eim
                are, aim = are * tre - aim * tim, are * tim + aim * tre
                d *= 2
            edge = 0 if reverse else CHUNKS - 1
            total = [a[edge:edge + 1, :] for a in (ere, eim, are, aim)]
            enter = [shifted(ere, 1, 0.0), shifted(eim, 1, 0.0), shifted(are, 1, 1.0), shifted(aim, 1, 0.0)]
            return enter, total

        def send_carry(l, way, q, enter, total):
            msg, buf = v.ca_msg[l][way][q], v.ca_buf[l][way][q]
            msg[0:1, 0:SN] = total[0]
            msg[0:1, SN:] = total[1]
            msg[1:2, 0:SN] = total[2]
            msg[1:2, SN:] = total[3]
            v.cin[l][q, 0, :, 0:SN] = enter[0]
            v.cin[l][q, 0, :, SN:] = enter[1]
            v.cin[l][q, 1, :, 0:SN] = enter[2]
            v.cin[l][q, 1, :, SN:] = enter[3]
            buf[me_t] = msg[...]
            return send(STATE, msg, buf)

        def take_carry(l, way, q, got, reverse):
            got()
            buf = v.ca_buf[l][way][q]
            cre, cim = jnp.zeros((1, SN), F32), jnp.zeros((1, SN), F32)
            for j in (range(NT - 1, -1, -1) if reverse else range(NT)):
                before = (j > me_t) if reverse else (j < me_t)
                ere, eim = buf[j, 0:1, 0:SN], buf[j, 0:1, SN:]
                are, aim = buf[j, 1:2, 0:SN], buf[j, 1:2, SN:]
                nre, nim = are * cre - aim * cim + ere, are * cim + aim * cre + eim
                cre, cim = jnp.where(before, nre, cre), jnp.where(before, nim, cim)
            cin = v.cin[l]
            ere, eim = cin[q, 0, :, 0:SN], cin[q, 0, :, SN:]
            are, aim = cin[q, 1, :, 0:SN], cin[q, 1, :, SN:]
            return ere + are * cre - aim * cim, eim + are * cim + aim * cre

        def forward_step(l, q, nv, s, c):
            lre, lim, scale = lam(l)
            here = at_step(q, s)
            bre = v.proj[l][here, 0:SN] * scale
            bim = v.proj[l][here, SN:] * scale
            keep = s < nv
            cre, cim = c
            nre, nim = lre * cre - lim * cim + bre, lre * cim + lim * cre + bim
            return jnp.where(keep, nre, cre), jnp.where(keep, nim, cim)

        def scan_ends(l, q):
            reverse = l % 2 == 1
            nv = valid_count(q)
            zero = jnp.zeros((CHUNKS, SN), F32)
            ere, eim = steps(lambda s, c: forward_step(l, q, nv, s, c), (zero, zero), reverse)
            enter, total = chunk_scan(q, l, ere, eim, False, reverse)
            return send_carry(l, 0, q, enter, total)

        def scan_states(l, q, got):
            reverse = l % 2 == 1
            nv = valid_count(q)
            init = take_carry(l, 0, q, got, reverse)
            state, low = v.state[l], v.slow[l]
            edge = ST if reverse else 0
            state[q, edge * CHUNKS:(edge + 1) * CHUNKS, 0:SN] = init[0]
            state[q, edge * CHUNKS:(edge + 1) * CHUNKS, SN:] = init[1]

            def body(s, c):
                nre, nim = forward_step(l, q, nv, s, c)
                at = pl.ds(pl.multiple_of((s if reverse else s + 1) * CHUNKS, CHUNKS), CHUNKS)
                state[q, at, 0:SN] = nre
                state[q, at, SN:] = nim
                here = at_step(q, s)
                low[here, 0:SN] = nre.astype(BF16)
                low[here, SN:] = nim.astype(BF16)
                return nre, nim

            steps(body, init, reverse)

        def adjoint_step(l, q, nv, s, c):
            lre, lim, _ = lam(l)
            here = at_step(q, s)
            are = v.sgrad[here, 0:SN] + c[0]
            aim = v.sgrad[here, SN:] + c[1]
            keep = s < nv
            nre, nim = lre * are + lim * aim, lre * aim - lim * are
            return (are, aim), keep, (jnp.where(keep, nre, are), jnp.where(keep, nim, aim))

        def adjoint_ends(l, q):
            reverse = l % 2 == 0
            nv = valid_count(q)
            zero = jnp.zeros((CHUNKS, SN), F32)
            ere, eim = steps(lambda s, c: adjoint_step(l, q, nv, s, c)[2], (zero, zero), reverse)
            enter, total = chunk_scan(q, l, ere, eim, True, reverse)
            return send_carry(l, 1, q, enter, total)

        def adjoint_states(l, q, got, sums):
            reverse = l % 2 == 0
            nv = valid_count(q)
            init = take_carry(l, 1, q, got, reverse)
            state, proj = v.state[l], v.proj[l]
            _, _, scale = lam(l)

            def body(s, c):
                w, (gre, gim, gsc) = c
                (are, aim), keep, w = adjoint_step(l, q, nv, s, w)
                are, aim = jnp.where(keep, are, 0.0), jnp.where(keep, aim, 0.0)
                here = at_step(q, s)
                v.mlow[here, 0:SN] = (are * scale).astype(BF16)
                v.mlow[here, SN:] = (aim * scale).astype(BF16)
                at = pl.ds(pl.multiple_of((s if reverse else s + 1) * CHUNKS, CHUNKS), CHUNKS)
                pre, pim = state[q, at, 0:SN], state[q, at, SN:]
                gre = gre + are * pre + aim * pim
                gim = gim + aim * pre - are * pim
                gsc = gsc + are * proj[here, 0:SN] + aim * proj[here, SN:]
                return w, (gre, gim, gsc)

            return steps(body, (init, sums), reverse)[1]

        class Reduce:
            def __init__(self, refs, rr, cc, whole, turned):
                self.own, self.s, self.r, self.res = refs
                self.whole = whole
                self.axes = [CORE, Y, X, Z] if turned else [CORE, X, Y, Z]
                self.size = [rr // 2]
                for n, _, _ in self.axes[1:]:
                    self.size.append(self.size[-1] // n)
                self.split = self.size[3] % 16 == 0
                self.base = [0]
                for (_, coord, _), size in zip(self.axes[1:], self.size[1:]):
                    self.base.append(self.base[-1] + coord * size)
                self.stage = 0
                self.last = 8 if whole else 6
                self.got, self.sent = None, None

            def start(self):
                r = self.r[0]
                self.got, self.sent = exchange(CORE, lambda p, k: self.s, lambda c, k: r.at[0], lambda n: r)

            def rows(self, ref, start, count):
                return ref.at[pl.ds(pl.multiple_of(start, 8), count), :]

            def come(self, level, start, count):
                total = self.rows(self.own, self.base[level] + start, count)[...]
                n = self.axes[level][0]
                for k in range(n - 1):
                    total = total + self.r[level][k, pl.ds(pl.multiple_of(start, 8), count), :].astype(F32)
                return total

            def scatter(self, level):
                n, coord, _ = self.axes[level]
                size, r = self.size[level], self.r[level]
                self.sent()
                for k in range(n):
                    p = lax.rem(coord + k, n)
                    total = self.come(level - 1, p * size, size)
                    if k == 0:
                        self.rows(self.own, self.base[level - 1] + p * size, size)[...] = total
                    else:
                        self.rows(self.s, (k - 1) * size, size)[...] = total.astype(BF16)
                self.got, self.sent = exchange(
                    self.axes[level], lambda p, k: self.rows(self.s, (k - 1) * size, size),
                    lambda c, k: r.at[k - 1], lambda m: r)

            def place(self, level):
                if self.whole:
                    at = core * self.size[0] + self.base[level]
                else:
                    at = my * self.size[2] + (self.base[3] - self.base[2] if level == 3 else 0)
                return self.rows(self.res, at, self.size[level])

            def gather(self, level):
                spot, r = self.place(level), self.r[level]
                self.got, self.sent = exchange(
                    self.axes[level], lambda p, k: spot, lambda c, k: spot, lambda m: r)

            def step(self):
                k = self.stage
                self.stage += 1
                if self.got is not None:
                    self.got()
                    self.got = None
                if k < 2 or (k == 2 and self.split):
                    self.scatter(k + 1)
                elif k == 2:
                    size, r = self.size[2], self.r[3]
                    self.sent()
                    spot = self.rows(self.s, 0, size)
                    spot[...] = self.come(2, 0, size).astype(BF16)
                    r[mz] = spot[...]
                    self.got, self.sent = exchange(
                        Z, lambda p, j: spot, lambda c, j: r.at[c], lambda m: r.at[pl.ds(0, m)])
                elif k == 3 and self.split:
                    self.place(3)[...] = self.come(3, 0, self.size[3]).astype(BF16)
                    self.gather(3)
                elif k == 3:
                    self.place(2)[...] = jnp.sum(self.r[3][...].astype(F32), axis=0).astype(BF16)
                elif k == 4:
                    if self.whole or self.axes[2] is Y:
                        self.gather(2)
                    else:
                        spot = self.place(2)
                        self.got, self.sent = exchange(
                            Y, lambda p, j: spot, lambda c, j: spot, lambda m: self.rows(self.res, 0, m * self.size[2]))
                elif k == 5 and self.whole:
                    self.gather(1)
                elif k == 6 and self.whole:
                    self.gather(0)

        reducers = [
            [[Reduce(v.red[l][k][half], *kinds[k], half == 1) for half in range(2)] for k in range(3)] for l in range(2)
        ]

        def glu_gradient(l):
            h, w = D // 2, E // 2
            for which in (0, 1):
                at = pl.ds(pl.multiple_of((core if which else 1 - core) * h, 128), h)
                for half, red in enumerate(reducers[l][0]):
                    part = dot_tn(v.hid[l][:, at], v.bothg[:, half * w:(half + 1) * w])
                    if which:
                        red.own[...] = part
                    else:
                        red.s[...] = part.astype(BF16)
                        red.start()

        def state_matrix_gradient(pair, left, right):
            p = 2 * NL // NY
            unit = min(p, NL)
            for c in range(2):
                v.full[...] = dot_tn(left[:, c * SN:(c + 1) * SN], right[...])
                for half, red in enumerate(pair):
                    cols = slice(half * (D // 2), (half + 1) * (D // 2))
                    for x in range(NX):
                        for part in range(NL // unit):
                            j = c * NL + part * unit
                            dst = ((j // p) * NX + x) * p + j % p if half else x * 2 * NL + j
                            mine = pl.ds(pl.multiple_of((x * 2 + core) * NL + part * unit, 8), unit)
                            theirs = pl.ds(pl.multiple_of((x * 2 + 1 - core) * NL + part * unit, 8), unit)
                            red.s[dst:dst + unit, :] = v.full[theirs, cols].astype(BF16)
                            red.own[dst:dst + unit, :] = v.full[mine, cols]
            for red in pair:
                red.start()

        def take_flat(dst):
            v.flat[...] = v.raw[...].astype(F32)

            def body(s, c):
                for q in range(Q):
                    for j in range(LT):
                        part = v.flat[pl.ds(s * (LT * Q) + j * Q + q, CHUNKS, stride=ST * LT * Q), :]
                        dst[at_step(q, s), j * 128:(j + 1) * 128] = part.astype(BF16)
                return c

            lax.fori_loop(0, ST, body, 0)

        def put_flat(r, q, tile):
            for i in range(RT // CHUNKS):
                for j in range(LT):
                    v.flat[pl.ds((r // CHUNKS + i) * (LT * Q) + j * Q + q, CHUNKS, stride=ST * LT * Q), :] = (
                        tile[i * CHUNKS:(i + 1) * CHUNKS, j * 128:(j + 1) * 128])

        def weight(ref):
            return ref[...].reshape(SL2, D)

        def forward_tile(l, r):
            at = pl.ds(r, RT)
            u = read_u(l)(r)
            _, normed = normalise(l, u)
            mixed = dot_nn(v.slow[l][at, :], weight(v.wout[l]))
            x = mixed + skip_ref[l:l + 1, :] * normed
            x2 = x * x
            t = jnp.tanh(x * (GELU_A + (GELU_A * GELU_B) * x2))
            half = 0.5 * (1.0 + t)
            hidden = (x * half).astype(BF16)
            v.hid[l][at, :] = hidden
            dgelu = half + (0.5 * x) * (1.0 - t * t) * (GELU_A + (3.0 * GELU_A * GELU_B) * x2)
            both = dot_nn(hidden, v.wglu[l])
            linear = both[:, :D]
            gate = 0.5 + 0.5 * jnp.tanh(0.5 * both[:, D:])
            return u, normed, dgelu, linear, gate

        def backward_tile(l, r, upstream, normed, dgelu, linear, gate):
            at = pl.ds(r, RT)
            pass_gate = upstream * gate
            bothg = jnp.concatenate([pass_gate, pass_gate * linear * (1.0 - gate)], axis=1).astype(BF16)
            v.bothg[at, :] = bothg
            preg = dot_nt(bothg, v.wglu[l]) * dgelu
            v.preg[at, :] = preg
            mlow = preg.astype(BF16)
            v.mlow[at, :] = mlow
            v.sgrad[at, :] = dot_nt(mlow, weight(v.wout[l]))
            return fold8(preg * normed)

        def norm_grads(l, q, sums):
            def body(r, c):
                at = pl.ds(r + q * L, RT)
                standard, _ = normalise(l, read_u(l)(r + q * L))
                ng = v.preg[at, :] * skip_ref[l:l + 1, :] + dot_nn(v.mlow[at, :], weight(v.win[l]))
                v.preg[at, :] = ng
                return c[0] + fold8(ng), c[1] + fold8(ng * standard)
            return tiles(body, sums, TILES)

        def send_norm_grads(l, sums):
            msg, buf = v.bw_msg[l], v.bw_buf[l]
            msg[0:1, :] = fold1(sums[0])
            msg[1:2, :] = fold1(sums[1])
            buf[me] = msg[...]
            return send(ALL, msg, buf)

        def put_small(l, skip, chain):
            msg, r = v.sm_msg, 4 * l
            msg[r:r + 1, :] = fold1(skip)
            msg[r + 1:r + 2, 0:SN] = fold1(chain[0])
            msg[r + 1:r + 2, SN:] = fold1(chain[1])
            msg[r + 2:r + 3, 0:SN] = fold1(chain[2])
            msg[r + 2:r + 3, SN:] = jnp.zeros((1, SN), F32)
            msg[r + 3:r + 4, :] = jnp.zeros((1, D), F32)

        def send_small():
            v.sm_buf[me_t] = v.sm_msg[...]
            return send(STATE, v.sm_msg, v.sm_buf)

        def pass_small(got):
            got()
            v.sm_sum[...] = jnp.sum(v.sm_buf[...], axis=0)
            v.sm_all[me_s] = v.sm_sum[...]
            return send(SEQ, v.sm_sum, v.sm_all)

        def take_norm_grads(l, got):
            got()
            buf = v.bw_buf[l]
            total = jnp.sum(buf[...], axis=0)
            v.small[l][0:2, :] = total

        def take_small(got):
            got()
            total = jnp.sum(v.sm_all[...], axis=0)
            out = v.result
            out[...] = jnp.zeros((16, D), F32)

            def mine(row):
                held = jnp.zeros((1, NL), F32)
                for j in range(NT):
                    held = jnp.where(me_t == j, row[:, j * NL:(j + 1) * NL], held)
                return held

            for l in range(2):
                out[l:l + 1, :] = v.small[l][1:2, :]
                out[2 + l:3 + l, :] = v.small[l][0:1, :]
                out[4 + l:5 + l, :] = total[4 * l:4 * l + 1, :]
                sum_re = mine(total[4 * l + 1:4 * l + 2, 0:SN])
                sum_im = mine(total[4 * l + 1:4 * l + 2, SN:])
                sum_sc = mine(total[4 * l + 2:4 * l + 3, 0:SN])
                own = slice(l, l + 1)
                rate = jnp.exp(nu_ref[own, :])
                phase = jnp.exp(theta_ref[own, :])
                lre, lim = v.par_msg[3 * l:3 * l + 1, 0:NL], v.par_msg[3 * l + 1:3 * l + 2, 0:NL]
                slow = jnp.tanh(rate)
                root = jnp.sqrt(2.0 * slow / (1.0 + slow))
                rate_grad = sum_sc * gamma_ref[own, :] * jnp.exp(-2.0 * rate) / root - (sum_re * lre + sum_im * lim)
                out[6 + l:7 + l, 0:NL] = rate * rate_grad
                out[8 + l:9 + l, 0:NL] = phase * (sum_im * lre - sum_re * lim)
                out[10 + l:11 + l, 0:NL] = sum_sc * root

        def input_gradient(l, r, upstream):
            stat, small = v.stat[l], v.small[l]
            standard, _ = normalise(l, read_u(l)(r))
            m = rep(v.mask[pl.ds(r, RT), :])
            inner = small[0:1, :] + standard * small[1:2, :]
            ng = v.preg[pl.ds(r, RT), :] - m * inner / stat[2:3, :]
            return upstream + stat[1:2, :] * gain_ref[l:l + 1, :] * ng

        rate = jnp.exp(nu_ref[...])
        phase = jnp.exp(theta_ref[...])
        modulus = jnp.exp(-rate)
        lam_re, lam_im = modulus * jnp.cos(phase), modulus * jnp.sin(phase)
        slow = jnp.tanh(rate)
        root = jnp.sqrt(2.0 * slow / (1.0 + slow))
        scale_own = gamma_ref[...] * root
        v.par_msg[...] = jnp.zeros((8, 128), F32)
        v.len_msg[...] = jnp.zeros((8, 128), F32)
        for l in range(2):
            for i, row in enumerate((lam_re, lam_im, scale_own)):
                v.par_msg[3 * l + i:3 * l + i + 1, 0:NL] = row[l:l + 1, :]
        v.par_buf[me_t] = v.par_msg[...]
        for q in range(Q):
            v.len_msg[q:q + 1, :] = jnp.full((1, 128), 1.0, F32) * len_ref[q].astype(F32)
        v.len_buf[me_s] = v.len_msg[...]

        base = me_t * L
        row = lax.broadcasted_iota(jnp.int32, (L, 128), 0)
        token = base + lax.rem(row, CHUNKS) * ST + row // CHUNKS
        count_own = jnp.float32(0)
        for q in range(Q):
            v.mask[q * L:(q + 1) * L, :] = (token < len_ref[q]).astype(F32)
            count_own = count_own + jnp.clip(len_ref[q] - base, 0, L).astype(F32)

        got_x()
        take_flat(v.x0)
        got_cot = load(cot_hbm, v.raw)
        local_stats(read_u(0), 0)
        for wait in got_own:
            wait()
        pl.semaphore_wait(barrier, N - 1)
        got_len = send(SEQ, v.len_msg, v.len_buf)
        got = send(ALL, v.st_msg[0], v.st_buf[0])
        got_par = send(STATE, v.par_msg, v.par_buf)
        gathers = [[Gather(v.win[0])], []]
        got_par()
        v.par[...] = jnp.concatenate([v.par_buf[j, :, 0:NL] for j in range(NT)], axis=1)
        chunk_powers(0)
        chunk_powers(1)
        take_counts()
        gathers[0].append(Gather(v.wout[0]))
        gathers[0][0].relay()
        global_stats(0, got)
        gathers[0][1].relay()

        def project(l, q):
            def body(r, c):
                at = pl.ds(r + q * L, RT)
                _, normed = normalise(l, read_u(l)(r + q * L))
                low = normed.astype(BF16)
                v.nlow[l][at, :] = low
                v.proj[l][at, :] = dot_nt(low, weight(v.win[l]))
                return c
            tiles(body, 0, TILES)

        def forward_scan(l, between):
            gathers[l][0].take()
            waits = []
            for q in range(Q):
                project(l, q)
                waits.append(scan_ends(l, q))
            gathers[l][1].take()
            v.wout[l][1] = -v.wout[l][1]
            between()
            return waits

        def more_weights():
            gathers[1].append(Gather(v.win[1]))
            gathers[1].append(Gather(v.wout[1]))

        waits = forward_scan(0, lambda: None)
        got_glu()
        total = zero8
        for q in range(Q):
            scan_states(0, q, waits[q])
            if q == 0:
                more_weights()

            def body(r, acc, q=q):
                at = pl.ds(r + q * L, RT)
                u, normed, dgelu, linear, gate = forward_tile(0, r + q * L)
                v.dgelu[at, :] = dgelu
                v.lin[at, :] = linear
                v.gate[at, :] = gate
                u = u + linear * gate
                v.u1[at, :] = u
                return acc + fold8(u * rep(v.mask[at, :]))

            total = tiles(body, total, TILES)

        local_stats(read_u(1), 1, total)
        got = send(ALL, v.st_msg[1], v.st_buf[1])
        got_cot()
        take_flat(v.cot)
        gathers[1][0].relay()
        gathers[1][1].relay()
        global_stats(1, got)
        waits = forward_scan(1, lambda: None)
        skip = zero8
        waits_b = []
        for q in range(Q):
            scan_states(1, q, waits[q])

            def body(r, acc, q=q):
                at = pl.ds(r + q * L, RT)
                u, normed, dgelu, linear, gate = forward_tile(1, r + q * L)
                v.up[at, :] = u + linear * gate
                upstream = v.cot[at, :].astype(F32)
                return acc + backward_tile(1, r + q * L, upstream, normed, dgelu, linear, gate)

            skip = tiles(body, skip, TILES)
            waits_b.append(adjoint_ends(1, q))

        def advance(*which):
            for pair in which:
                for red in pair:
                    if red.stage < red.last:
                        red.step()

        def mixer_gradients(l, point):
            glu_gradient(l)
            advance(*plan[point])
            state_matrix_gradient(reducers[l][1], v.slow[l], v.mlow)
            advance(*plan[point + 1])

        def input_matrix_gradient(l):
            state_matrix_gradient(reducers[l][2], v.mlow, v.nlow[l])

        (g0, o0, i0), (g1, o1, i1) = reducers
        plan = [(), (g1,), (o1,), (), (g1,i1,o1,), (), (g1,o1,i1,), (), (), (g0,i1,), (), (o0,g1,o1,), (), (i0,g0,o0,i1,o1,g1,i1,), (), (g0,i0,g1,), (), ]
        stored = []

        mixer_gradients(1, 0)
        chain = (jnp.zeros((CHUNKS, SN), F32),) * 3
        sums = (zero8, zero8)
        for q in range(Q):
            chain = adjoint_states(1, q, waits_b[q], chain)
            sums = norm_grads(1, q, sums)
            if q == 0:
                advance(*plan[2])
        put_small(1, skip, chain)
        got = send_norm_grads(1, sums)
        input_matrix_gradient(1)
        advance(*plan[3])
        for q in range(Q):
            def body(r, c, q=q):
                put_flat(r, q, v.up[pl.ds(r + q * L, RT), :])
                return c
            tiles(body, 0, TILES)
        stored.append(load(v.flat, u2_out))
        advance(*plan[4])
        take_norm_grads(1, got)
        advance(*plan[5])

        skip = zero8
        waits_b = []
        for q in range(Q):
            def body(r, acc, q=q):
                at = pl.ds(r + q * L, RT)
                upstream = input_gradient(1, r + q * L, v.cot[at, :].astype(F32))
                v.up[at, :] = upstream
                _, normed = normalise(0, read_u(0)(r + q * L))
                return acc + backward_tile(0, r + q * L, upstream, normed, v.dgelu[at, :], v.lin[at, :], v.gate[at, :])

            skip = tiles(body, skip, TILES)
            waits_b.append(adjoint_ends(0, q))
            advance(*plan[6 + min(q, 1)])
        mixer_gradients(0, 8)
        chain = (jnp.zeros((CHUNKS, SN), F32),) * 3
        for q in range(Q):
            chain = adjoint_states(0, q, waits_b[q], chain)
        put_small(0, skip, chain)
        advance(*plan[10])
        input_matrix_gradient(0)
        got_small = send_small()
        advance(*plan[11])
        sums = (zero8, zero8)
        for q in range(Q):
            sums = norm_grads(0, q, sums)
            if q == 0:
                advance(*plan[12])
        got = send_norm_grads(0, sums)
        advance(*plan[13])
        take_norm_grads(0, got)
        advance(*plan[15])
        got_small = pass_small(got_small)
        stored[0]()

        for q in range(Q):
            def body(r, c, q=q):
                put_flat(r, q, input_gradient(0, r + q * L, v.up[pl.ds(r + q * L, RT), :]))
                return c

            tiles(body, 0, TILES)
        stored = [load(v.flat, ig_out)]
        advance(*plan[16])
        take_small(got_small)
        stored.append(load(v.result, small_out))
        order = [g0, i0, o0, g1, o1, i1]
        while any(pair[0].stage < pair[0].last for pair in order):
            for pair in order:
                advance(pair)
        for l in range(2):
            for half in range(2):
                stored.append(load(reducers[l][0][half].res, glu_out.at[l, half]))
                stored.append(load(reducers[l][1][half].res, out_out.at[l, half]))
                stored.append(load(reducers[l][2][half].res, int_out.at[l, half]))
        for w in pending:
            w()

    out_shape = [
        jax.ShapeDtypeStruct((FLAT, 128), F32),
        jax.ShapeDtypeStruct((FLAT, 128), F32),
        jax.ShapeDtypeStruct((16, D), F32),
        jax.ShapeDtypeStruct((2, 2, 2 * NL, D // 2), BF16),
        jax.ShapeDtypeStruct((2, 2, 2 * NL, D // 2), BF16),
        jax.ShapeDtypeStruct((2, 2, D, E // 2), BF16),
    ]
    hbm = pl.BlockSpec(memory_space=pl.ANY)
    vmem = pl.BlockSpec(memory_space=pltpu.VMEM)
    smem = pl.BlockSpec(memory_space=pltpu.SMEM)
    return pl.pallas_call(
        kernel,
        out_shape=out_shape,
        in_specs=[hbm, hbm, smem] + [vmem] * 6 + [hbm] * 3,
        out_specs=[hbm] * 6,
        scratch_shapes=scratch,
        compiler_params=pltpu.CompilerParams(
            collective_id=0, has_side_effects=True, vmem_limit_bytes=VMEM_LIMIT
        ),
    )


def finish(rows, seqs, width, own):
    D, NL = width, own
    FLAT = rows * seqs * D // 128

    def kernel(u2, ig, small, ing, outg, glu, u2_o, ig_o, gain_o, bias_o, skip_o, nu_o, theta_o, gamma_o, in_o, out_o, glu_o,
               wide, glu_low, glu_wide, in_low, out_low, in_wide, out_wide, sems):
        count = []

        def copy(src, dst):
            c = pltpu.make_async_copy(src, dst, sems.at[len(count)])
            count.append(c)
            c.start()
            return c

        got_glu = [copy(glu.at[l], glu_low.at[l]) for l in range(2)]
        got_u2, got_ig = copy(u2, wide.at[0]), copy(ig, wide.at[1])
        got_in, got_out = copy(ing, in_low), copy(outg, out_low)
        back = []
        for l in range(2):
            got_glu[l].wait()
            for half in range(2):
                glu_wide[l, :, half * D:(half + 1) * D] = glu_low[l, half].astype(F32)
            back.append(copy(glu_wide.at[l], glu_o.at[l]))
        got_u2.wait()
        back.append(copy(wide.at[0], u2_o))
        got_ig.wait()
        back.append(copy(wide.at[1], ig_o))
        got_in.wait()
        got_out.wait()
        for l in range(2):
            for half in range(2):
                cols = slice(half * (D // 2), (half + 1) * (D // 2))
                for c in range(2):
                    part = out_low[l, half, c * NL:(c + 1) * NL, :].astype(F32)
                    out_wide[l, c, :, cols] = -part if c else part
                    in_wide[l, c, :, cols] = in_low[l, half, c * NL:(c + 1) * NL, :].astype(F32)
        back += [copy(in_wide, in_o), copy(out_wide, out_o)]
        for l in range(2):
            for ref, at in ((gain_o, 0), (bias_o, 2), (skip_o, 4)):
                ref[l:l + 1, :] = small[at + l:at + l + 1, :]
            for ref, at in ((nu_o, 6), (theta_o, 8), (gamma_o, 10)):
                ref[l:l + 1, :] = small[at + l:at + l + 1, 0:NL]
        for b in back:
            b.wait()

    f32 = lambda *shape: jax.ShapeDtypeStruct(shape, F32)
    hbm = pl.BlockSpec(memory_space=pl.ANY)
    vmem = pl.BlockSpec(memory_space=pltpu.VMEM)
    return pl.pallas_call(
        kernel,
        out_shape=[f32(FLAT, 128), f32(FLAT, 128)] + [f32(2, D)] * 3 + [f32(2, NL)] * 3
        + [f32(2, 2, NL, D), f32(2, 2, NL, D), f32(2, D, 2 * D)],
        in_specs=[hbm, hbm, vmem] + [hbm] * 3,
        out_specs=[hbm, hbm] + [vmem] * 6 + [hbm] * 3,
        scratch_shapes=[
            pltpu.VMEM((2, FLAT, 128), F32),
            pltpu.VMEM((2, 2, D, D), BF16),
            pltpu.VMEM((2, D, 2 * D), F32),
            pltpu.VMEM((2, 2, 2 * NL, D // 2), BF16),
            pltpu.VMEM((2, 2, 2 * NL, D // 2), BF16),
            pltpu.VMEM((2, 2, NL, D), F32),
            pltpu.VMEM((2, 2, NL, D), F32),
            pltpu.SemaphoreType.DMA((12,)),
        ],
        compiler_params=pltpu.CompilerParams(vmem_limit_bytes=VMEM_LIMIT),
    )


def solution(mesh):
    seq_devices, state_devices = mesh.shape["seq"], mesh.shape["state"]

    def per_device(
        inputs, lengths, norm_gain, norm_bias, in_proj, out_proj,
        nu_log, theta_log, gamma_gain, skip_gain, glu_weight, cotangent,
    ):
        rows, seqs, width = inputs.shape
        layers, own = nu_log.shape
        lanes = width // 128

        def flat(a):
            a = a.reshape(rows, seqs, lanes, 128).transpose(0, 2, 1, 3)
            return a.reshape(rows * seqs * lanes, 128)

        def by_tokens(a):
            a = a.reshape(rows, lanes, seqs, 128).transpose(0, 2, 1, 3)
            return a.reshape(rows, seqs, width)

        step = build(seq_devices, state_devices, rows, seqs, width, own, layers)
        held = step(
            flat(inputs), flat(cotangent), lengths, norm_gain, norm_bias, nu_log, theta_log, gamma_gain, skip_gain,
            jnp.swapaxes(in_proj, 2, 3), out_proj, glu_weight,
        )
        u2, input_grad, gain, bias, skip, nu, theta, gamma, in_grad, out_grad, glu = finish(rows, seqs, width, own)(*held)
        return by_tokens(u2), by_tokens(input_grad), gain, bias, jnp.swapaxes(in_grad, 2, 3), out_grad, nu, theta, gamma, skip, glu

    return jax.shard_map(
        per_device,
        mesh=mesh,
        in_specs=(
            P("state", "seq", None),
            P("seq"),
            P(),
            P(),
            P(None, None, None, "state"),
            P(None, None, "state", None),
            P(None, "state"),
            P(None, "state"),
            P(None, "state"),
            P(),
            P(),
            P("state", "seq", None),
        ),
        out_specs=(
            P("state", "seq", None),
            P("state", "seq", None),
            P(),
            P(),
            P(None, None, None, "state"),
            P(None, None, "state", None),
            P(None, "state"),
            P(None, "state"),
            P(None, "state"),
            P(),
            P(),
        ),
        check_vma=False,
    )
```

```python
import math

import jax
import jax.numpy as jnp
from jax import lax
from jax.experimental import pallas as pl
from jax.experimental.pallas import tpu as pltpu
from jax.sharding import PartitionSpec as P

EPSILON = 1e-05
MESH = pl.DeviceIdType.MESH
F32 = jnp.float32
BF16 = jnp.bfloat16
CHUNKS = 16
GELU_A = math.sqrt(2.0 / math.pi)
GELU_B = 0.044715
VMEM_LIMIT = 65280 * 1024


def dot_nn(a, b):
    return lax.dot_general(a, b, (((1,), (0,)), ((), ())), preferred_element_type=F32)


def dot_nt(a, b):
    return lax.dot_general(a, b, (((1,), (1,)), ((), ())), preferred_element_type=F32)


def dot_tn(a, b):
    return lax.dot_general(a, b, (((0,), (0,)), ((), ())), preferred_element_type=F32)


class Buffers:
    def __init__(self):
        self.shapes = []

    def add(self, shape, dtype):
        self.shapes.append(pltpu.VMEM(shape, dtype))
        return len(self.shapes) - 1

    def bind(self, refs):
        bound = Buffers()
        for key, places in vars(self).items():
            if places is not self.shapes:
                setattr(bound, key, jax.tree.map(lambda i: refs[i], places))
        return bound


def build(axis_seq, axis_state, rows, seqs, width, states_own, layers):
    NS, NT = axis_seq, axis_state
    N = NS * NT
    NX = NT // 2
    NY = NX if NS % NX == 0 else 1
    NZ = NS // NY
    L, Q, D, NL = rows, seqs, width, states_own
    ST = L // CHUNKS
    SN = NL * NT
    SL2 = 2 * SN
    E = 2 * D
    T = Q * L
    RT = min(512, L)
    TILES = L // RT
    UN = 4
    assert layers == 2 and NT % 2 == 0 and L % CHUNKS == 0

    v = Buffers()
    vm = v.add
    LT = D // 128
    FLAT = T * LT
    v.raw = vm((FLAT, 128), BF16)
    v.flat = vm((FLAT + ST * LT * Q, 128), F32)
    v.x0 = vm((T, D), BF16)
    v.cot = vm((T, D), BF16)
    v.u1 = vm((T, D), F32)
    v.mask = vm((T, 128), F32)
    v.nlow, v.slow, v.hid = ([vm((T, D), BF16) for _ in range(2)] for _ in range(3))
    v.proj = [vm((T, SL2), F32) for _ in range(2)]
    v.state = [vm((Q, (ST + 1) * CHUNKS, SL2), F32) for _ in range(2)]
    v.apow = [vm((Q, 2, CHUNKS, SN), F32) for _ in range(2)]
    v.cin = [vm((Q, 2, CHUNKS, SL2), F32) for _ in range(2)]
    v.win, v.wout = ([vm((2, NT, NL, D), BF16) for _ in range(2)] for _ in range(2))
    v.st_msg, v.bw_msg = ([vm((2, D), F32) for _ in range(2)] for _ in range(2))
    v.st_buf, v.bw_buf = ([vm((N, 2, D), F32) for _ in range(2)] for _ in range(2))
    v.len_msg = vm((8, 128), F32)
    v.len_buf = vm((NS, 8, 128), F32)
    v.sm_msg = vm((8, D), F32)
    v.sm_buf = vm((NT, 8, D), F32)
    v.sm_sum = vm((8, D), F32)
    v.sm_all = vm((NS, 8, D), F32)
    v.stat, v.small = ([vm((8, D), F32) for _ in range(2)] for _ in range(2))
    v.ca_msg = [[[vm((2, SL2), F32) for _ in range(Q)] for _ in range(2)] for _ in range(2)]
    v.ca_buf = [[[vm((NT, 2, SL2), F32) for _ in range(Q)] for _ in range(2)] for _ in range(2)]
    v.dgelu, v.lin, v.gate, v.preg, v.up = (vm((T, D), F32) for _ in range(5))
    v.wglu = vm((2, D, E), BF16)
    v.bothg = vm((T, E), BF16)
    v.mlow = vm((T, D), BF16)
    v.sgrad = vm((T, SL2), F32)
    v.par_msg = vm((8, 128), F32)
    v.par_buf = vm((NT, 8, 128), F32)
    v.par = vm((8, SN), F32)
    v.result = vm((16, D), F32)
    v.counts = vm((N, 1, D), F32)
    v.full = vm((SN, D), F32)

    def reduce_buffers(rr, cc, whole, turned):
        h = rr // 2
        n1, n2 = (NY, NX) if turned else (NX, NY)
        p1 = h // n1
        p2 = p1 // n2
        p3 = p2 // NZ
        last = (NZ - 1, p3, cc) if p3 % 16 == 0 else (NZ, p2, cc)
        return [
            vm((h, cc), F32),
            vm((h, cc), BF16),
            [vm((1, h, cc), BF16), vm((max(n1 - 1, 1), p1, cc), BF16), vm((max(n2 - 1, 1), p2, cc), BF16), vm(last, BF16)],
            vm((rr if whole else 2 * NL, cc), BF16),
        ]

    kinds = [(D, E // 2, True), (SL2, D // 2, False), (SL2, D // 2, False)]
    v.red = [[[reduce_buffers(*kind, turned) for turned in (False, True)] for kind in kinds] for _ in range(2)]
    places = v
    SEMS = 160
    scratch = v.shapes + [
        pltpu.SemaphoreType.DMA((SEMS,)),
        pltpu.SemaphoreType.DMA((SEMS,)),
        pltpu.SemaphoreType.DMA((SEMS,)),
    ]

    def kernel(
        x_hbm, cot_hbm, len_ref, gain_ref, bias_ref, nu_ref, theta_ref, gamma_ref, skip_ref, win_hbm, wout_hbm, glu_hbm,
        u2_out, ig_out, small_out, int_out, out_out, glu_out, *rest,
    ):
        v = places.bind(rest[: len(places.shapes)])
        ssem, rsem, lsem = rest[len(places.shapes):]
        me_s, me_t = lax.axis_index("seq"), lax.axis_index("state")
        me = me_s * NT + me_t
        core, mx = lax.rem(me_t, 2), me_t // 2
        my, mz = lax.rem(me_s, NY), me_s // NY
        CORE = (2, core, lambda p: (me_s, mx * 2 + p))
        X = (NX, mx, lambda p: (me_s, p * 2 + core))
        Y = (NY, my, lambda p: (mz * NY + p, me_t))
        Z = (NZ, mz, lambda p: (p * NY + my, me_t))
        STATE = (NT, me_t, lambda p: (me_s, p))
        SEQ = (NS, me_s, lambda p: (p, me_t))
        ALL = (N, me, lambda p: (p // NT, lax.rem(p, NT)))
        remotes, locals_, pending = [], [], []

        def once(wait):
            left = [wait]
            pending.append(lambda: left.pop()() if left else None)
            return pending[-1]

        def wait_bytes(view, sem):
            pltpu.make_async_copy(view, view, sem).wait()

        def exchange(axis, src_of, dst_of, size_view):
            n, coord, dev = axis
            k = len(remotes)
            remotes.append(k)
            assert k < SEMS
            if n == 1:
                return once(lambda: None), once(lambda: None)

            def one(step):
                p = lax.rem(coord + step, n)
                pltpu.make_async_remote_copy(
                    src_ref=src_of(p, step), dst_ref=dst_of(coord, step), send_sem=ssem.at[k],
                    recv_sem=rsem.at[k], device_id=dev(p), device_id_type=MESH,
                ).start()

            if n <= 8:
                for step in range(1, n):
                    one(step)
            else:
                def body(step, c):
                    one(step)
                    return c
                lax.fori_loop(1, n, body, 0)
            return (
                once(lambda: wait_bytes(size_view(n - 1), rsem.at[k])),
                once(lambda: wait_bytes(size_view(n - 1), ssem.at[k])),
            )

        def send(axis, src, buf):
            return exchange(axis, lambda p, k: src, lambda c, k: buf.at[c], lambda n: buf.at[pl.ds(0, n)])[0]

        def load(src, dst):
            k = len(locals_)
            locals_.append(k)
            copy = pltpu.make_async_copy(src, dst, lsem.at[k])
            copy.start()
            return once(copy.wait)

        got_x = load(x_hbm, v.raw)
        got_own = [load(hbm.at[l], dst[l].at[:, me_t]) for l in range(2) for hbm, dst in ((win_hbm, v.win), (wout_hbm, v.wout))]
        got_glu = load(glu_hbm, v.wglu)

        barrier = pltpu.get_barrier_semaphore()

        def greet(step, c):
            p = lax.rem(me + step, N)
            pl.semaphore_signal(barrier, inc=1, device_id=(p // NT, lax.rem(p, NT)), device_id_type=MESH)
            return c

        lax.fori_loop(1, N, greet, 0)

        class Gather:
            def __init__(self, dst):
                self.dst = dst
                self.x = self.spread(X, me_t)
                self.rest = [self.spread(CORE, me_t)]

            def spread(self, axis, slot):
                spot = self.dst.at[:, slot]
                return exchange(axis, lambda p, k: spot, lambda c, k: spot, lambda n: self.dst.at[:, pl.ds(0, n)])

            def relay(self):
                self.x[0]()
                self.rest += [self.spread(CORE, lax.rem(mx + k, NX) * 2 + core) for k in range(1, NX)]

            def take(self):
                self.x[1]()
                for came, sent in self.rest:
                    came()
                    sent()

        def rep(m, w=D):
            return jnp.concatenate([m] * (w // 128), axis=1)

        def tiles(body, init, count=T // RT):
            return lax.fori_loop(0, count, lambda i, c: body(pl.multiple_of(i * RT, RT), c), init)

        def fold8(a):
            return jnp.sum(a.reshape(a.shape[0] // 8, 8, a.shape[1]), axis=0)

        def fold1(a):
            return jnp.sum(a, axis=0, keepdims=True)

        zero8 = jnp.zeros((8, D), F32)

        def local_stats(read, l, total=None):
            if total is None:
                def add(r, acc):
                    return acc + fold8(read(r) * rep(v.mask[pl.ds(r, RT), :]))
                total = tiles(add, zero8)
            mean_own = fold1(total) / jnp.maximum(count_own, 1.0)

            def spread(r, acc):
                c = read(r) - mean_own
                return acc + fold8(c * c * rep(v.mask[pl.ds(r, RT), :]))

            squares = fold1(tiles(spread, zero8))
            v.st_msg[l][0:1, :] = mean_own
            v.st_msg[l][1:2, :] = squares
            v.st_buf[l][me] = v.st_msg[l][...]

        def global_stats(l, got):
            got()
            buf = v.st_buf[l]
            means, squares = buf[:, 0:1, :], buf[:, 1:2, :]
            counts = v.counts[...]
            count = jnp.sum(counts, axis=0)
            mean = jnp.sum(means * counts, axis=0) / count
            off = means - mean[None]
            variance = jnp.sum(squares + counts * off * off, axis=0) / count
            stat = v.stat[l]
            stat[0:1, :] = mean
            stat[1:2, :] = lax.rsqrt(variance + EPSILON)
            stat[2:3, :] = count

        def take_counts():
            got_len()
            for s in range(NS):
                for t in range(NT):
                    held = jnp.zeros((1, 128), F32)
                    for q in range(Q):
                        held = held + jnp.clip(v.len_buf[s, q:q + 1, :] - float(t * L), 0.0, float(L))
                    v.counts[s * NT + t] = rep(held)

        def normalise(l, u):
            stat = v.stat[l]
            standard = (u - stat[0:1, :]) * stat[1:2, :]
            return standard, standard * gain_ref[l:l + 1, :] + bias_ref[l:l + 1, :]

        def read_u(l):
            if l == 0:
                return lambda r: v.x0[pl.ds(r, RT), :].astype(F32)
            return lambda r: v.u1[pl.ds(r, RT), :]

        def valid_count(q):
            chunk = lax.broadcasted_iota(jnp.int32, (CHUNKS, SN), 0)
            return jnp.clip(len_ref[q] - base - chunk * ST, 0, ST)

        def lam(l):
            return v.par[3 * l:3 * l + 1, :], v.par[3 * l + 1:3 * l + 2, :], v.par[3 * l + 2:3 * l + 3, :]

        def chunk_powers(l):
            for q in range(Q):
                nv = valid_count(q)
                lre, lim, _ = lam(l)
                lre = jnp.broadcast_to(lre, (CHUNKS, SN))
                lim = jnp.broadcast_to(lim, (CHUNKS, SN))
                pre, pim = jnp.ones((CHUNKS, SN), F32), jnp.zeros((CHUNKS, SN), F32)
                bit = 1
                while bit <= ST:
                    on = (nv & bit) != 0
                    nre, nim = pre * lre - pim * lim, pre * lim + pim * lre
                    pre, pim = jnp.where(on, nre, pre), jnp.where(on, nim, pim)
                    lre, lim = lre * lre - lim * lim, 2.0 * lre * lim
                    bit *= 2
                v.apow[l][q, 0] = pre
                v.apow[l][q, 1] = pim

        def steps(body, init, reverse):
            def outer(i, c):
                for j in range(UN):
                    s = i * UN + j
                    if reverse:
                        s = ST - 1 - s
                    c = body(s, c)
                return c
            return lax.fori_loop(0, ST // UN, outer, init)

        def at_step(q, s):
            return pl.ds(pl.multiple_of(q * L + s * CHUNKS, CHUNKS), CHUNKS)

        def chunk_scan(q, l, end_re, end_im, conj, reverse):
            are, aim = v.apow[l][q, 0], v.apow[l][q, 1]
            if conj:
                aim = -aim
            ere, eim = end_re, end_im
            chunk = lax.broadcasted_iota(jnp.int32, (CHUNKS, SN), 0)

            def shifted(a, d, fill):
                if reverse:
                    return jnp.where(chunk < CHUNKS - d, pltpu.roll(a, CHUNKS - d, 0), fill)
                return jnp.where(chunk >= d, pltpu.roll(a, d, 0), fill)

            d = 1
            while d < CHUNKS:
                sre, sim = shifted(ere, d, 0.0), shifted(eim, d, 0.0)
                tre, tim = shifted(are, d, 1.0), shifted(aim, d, 0.0)
                ere, eim = are * sre - aim * sim + ere, are * sim + aim * sre + eim
                are, aim = are * tre - aim * tim, are * tim + aim * tre
                d *= 2
            edge = 0 if reverse else CHUNKS - 1
            total = [a[edge:edge + 1, :] for a in (ere, eim, are, aim)]
            enter = [shifted(ere, 1, 0.0), shifted(eim, 1, 0.0), shifted(are, 1, 1.0), shifted(aim, 1, 0.0)]
            return enter, total

        def send_carry(l, way, q, enter, total):
            msg, buf = v.ca_msg[l][way][q], v.ca_buf[l][way][q]
            msg[0:1, 0:SN] = total[0]
            msg[0:1, SN:] = total[1]
            msg[1:2, 0:SN] = total[2]
            msg[1:2, SN:] = total[3]
            v.cin[l][q, 0, :, 0:SN] = enter[0]
            v.cin[l][q, 0, :, SN:] = enter[1]
            v.cin[l][q, 1, :, 0:SN] = enter[2]
            v.cin[l][q, 1, :, SN:] = enter[3]
            buf[me_t] = msg[...]
            return send(STATE, msg, buf)

        def take_carry(l, way, q, got, reverse):
            got()
            buf = v.ca_buf[l][way][q]
            cre, cim = jnp.zeros((1, SN), F32), jnp.zeros((1, SN), F32)
            for j in (range(NT - 1, -1, -1) if reverse else range(NT)):
                before = (j > me_t) if reverse else (j < me_t)
                ere, eim = buf[j, 0:1, 0:SN], buf[j, 0:1, SN:]
                are, aim = buf[j, 1:2, 0:SN], buf[j, 1:2, SN:]
                nre, nim = are * cre - aim * cim + ere, are * cim + aim * cre + eim
                cre, cim = jnp.where(before, nre, cre), jnp.where(before, nim, cim)
            cin = v.cin[l]
            ere, eim = cin[q, 0, :, 0:SN], cin[q, 0, :, SN:]
            are, aim = cin[q, 1, :, 0:SN], cin[q, 1, :, SN:]
            return ere + are * cre - aim * cim, eim + are * cim + aim * cre

        def forward_step(l, q, nv, s, c):
            lre, lim, scale = lam(l)
            here = at_step(q, s)
            bre = v.proj[l][here, 0:SN] * scale
            bim = v.proj[l][here, SN:] * scale
            keep = s < nv
            cre, cim = c
            nre, nim = lre * cre - lim * cim + bre, lre * cim + lim * cre + bim
            return jnp.where(keep, nre, cre), jnp.where(keep, nim, cim)

        def scan_ends(l, q):
            reverse = l % 2 == 1
            nv = valid_count(q)
            zero = jnp.zeros((CHUNKS, SN), F32)
            ere, eim = steps(lambda s, c: forward_step(l, q, nv, s, c), (zero, zero), reverse)
            enter, total = chunk_scan(q, l, ere, eim, False, reverse)
            return send_carry(l, 0, q, enter, total)

        def scan_states(l, q, got):
            reverse = l % 2 == 1
            nv = valid_count(q)
            init = take_carry(l, 0, q, got, reverse)
            state, low = v.state[l], v.slow[l]
            edge = ST if reverse else 0
            state[q, edge * CHUNKS:(edge + 1) * CHUNKS, 0:SN] = init[0]
            state[q, edge * CHUNKS:(edge + 1) * CHUNKS, SN:] = init[1]

            def body(s, c):
                nre, nim = forward_step(l, q, nv, s, c)
                at = pl.ds(pl.multiple_of((s if reverse else s + 1) * CHUNKS, CHUNKS), CHUNKS)
                state[q, at, 0:SN] = nre
                state[q, at, SN:] = nim
                here = at_step(q, s)
                low[here, 0:SN] = nre.astype(BF16)
                low[here, SN:] = nim.astype(BF16)
                return nre, nim

            steps(body, init, reverse)

        def adjoint_step(l, q, nv, s, c):
            lre, lim, _ = lam(l)
            here = at_step(q, s)
            are = v.sgrad[here, 0:SN] + c[0]
            aim = v.sgrad[here, SN:] + c[1]
            keep = s < nv
            nre, nim = lre * are + lim * aim, lre * aim - lim * are
            return (are, aim), keep, (jnp.where(keep, nre, are), jnp.where(keep, nim, aim))

        def adjoint_ends(l, q):
            reverse = l % 2 == 0
            nv = valid_count(q)
            zero = jnp.zeros((CHUNKS, SN), F32)
            ere, eim = steps(lambda s, c: adjoint_step(l, q, nv, s, c)[2], (zero, zero), reverse)
            enter, total = chunk_scan(q, l, ere, eim, True, reverse)
            return send_carry(l, 1, q, enter, total)

        def adjoint_states(l, q, got, sums):
            reverse = l % 2 == 0
            nv = valid_count(q)
            init = take_carry(l, 1, q, got, reverse)
            state, proj = v.state[l], v.proj[l]
            _, _, scale = lam(l)

            def body(s, c):
                w, (gre, gim, gsc) = c
                (are, aim), keep, w = adjoint_step(l, q, nv, s, w)
                are, aim = jnp.where(keep, are, 0.0), jnp.where(keep, aim, 0.0)
                here = at_step(q, s)
                v.mlow[here, 0:SN] = (are * scale).astype(BF16)
                v.mlow[here, SN:] = (aim * scale).astype(BF16)
                at = pl.ds(pl.multiple_of((s if reverse else s + 1) * CHUNKS, CHUNKS), CHUNKS)
                pre, pim = state[q, at, 0:SN], state[q, at, SN:]
                gre = gre + are * pre + aim * pim
                gim = gim + aim * pre - are * pim
                gsc = gsc + are * proj[here, 0:SN] + aim * proj[here, SN:]
                return w, (gre, gim, gsc)

            return steps(body, (init, sums), reverse)[1]

        class Reduce:
            def __init__(self, refs, rr, cc, whole, turned):
                self.own, self.s, self.r, self.res = refs
                self.whole = whole
                self.axes = [CORE, Y, X, Z] if turned else [CORE, X, Y, Z]
                self.size = [rr // 2]
                for n, _, _ in self.axes[1:]:
                    self.size.append(self.size[-1] // n)
                self.split = self.size[3] % 16 == 0
                self.base = [0]
                for (_, coord, _), size in zip(self.axes[1:], self.size[1:]):
                    self.base.append(self.base[-1] + coord * size)
                self.stage = 0
                self.last = 8 if whole else 6
                self.got, self.sent = None, None

            def start(self):
                r = self.r[0]
                self.got, self.sent = exchange(CORE, lambda p, k: self.s, lambda c, k: r.at[0], lambda n: r)

            def rows(self, ref, start, count):
                return ref.at[pl.ds(pl.multiple_of(start, 8), count), :]

            def come(self, level, start, count):
                total = self.rows(self.own, self.base[level] + start, count)[...]
                n = self.axes[level][0]
                for k in range(n - 1):
                    total = total + self.r[level][k, pl.ds(pl.multiple_of(start, 8), count), :].astype(F32)
                return total

            def scatter(self, level):
                n, coord, _ = self.axes[level]
                size, r = self.size[level], self.r[level]
                self.sent()
                for k in range(n):
                    p = lax.rem(coord + k, n)
                    total = self.come(level - 1, p * size, size)
                    if k == 0:
                        self.rows(self.own, self.base[level - 1] + p * size, size)[...] = total
                    else:
                        self.rows(self.s, (k - 1) * size, size)[...] = total.astype(BF16)
                self.got, self.sent = exchange(
                    self.axes[level], lambda p, k: self.rows(self.s, (k - 1) * size, size),
                    lambda c, k: r.at[k - 1], lambda m: r)

            def place(self, level):
                if self.whole:
                    at = core * self.size[0] + self.base[level]
                else:
                    at = my * self.size[2] + (self.base[3] - self.base[2] if level == 3 else 0)
                return self.rows(self.res, at, self.size[level])

            def gather(self, level):
                spot, r = self.place(level), self.r[level]
                self.got, self.sent = exchange(
                    self.axes[level], lambda p, k: spot, lambda c, k: spot, lambda m: r)

            def step(self):
                k = self.stage
                self.stage += 1
                if self.got is not None:
                    self.got()
                    self.got = None
                if k < 2 or (k == 2 and self.split):
                    self.scatter(k + 1)
                elif k == 2:
                    size, r = self.size[2], self.r[3]
                    self.sent()
                    spot = self.rows(self.s, 0, size)
                    spot[...] = self.come(2, 0, size).astype(BF16)
                    r[mz] = spot[...]
                    self.got, self.sent = exchange(
                        Z, lambda p, j: spot, lambda c, j: r.at[c], lambda m: r.at[pl.ds(0, m)])
                elif k == 3 and self.split:
                    self.place(3)[...] = self.come(3, 0, self.size[3]).astype(BF16)
                    self.gather(3)
                elif k == 3:
                    self.place(2)[...] = jnp.sum(self.r[3][...].astype(F32), axis=0).astype(BF16)
                elif k == 4:
                    if self.whole or self.axes[2] is Y:
                        self.gather(2)
                    else:
                        spot = self.place(2)
                        self.got, self.sent = exchange(
                            Y, lambda p, j: spot, lambda c, j: spot, lambda m: self.rows(self.res, 0, m * self.size[2]))
                elif k == 5 and self.whole:
                    self.gather(1)
                elif k == 6 and self.whole:
                    self.gather(0)

        reducers = [
            [[Reduce(v.red[l][k][half], *kinds[k], half == 1) for half in range(2)] for k in range(3)] for l in range(2)
        ]

        def glu_gradient(l):
            h, w = D // 2, E // 2
            for which in (0, 1):
                at = pl.ds(pl.multiple_of((core if which else 1 - core) * h, 128), h)
                for half, red in enumerate(reducers[l][0]):
                    part = dot_tn(v.hid[l][:, at], v.bothg[:, half * w:(half + 1) * w])
                    if which:
                        red.own[...] = part
                    else:
                        red.s[...] = part.astype(BF16)
                        red.start()

        def state_matrix_gradient(pair, left, right):
            p = 2 * NL // NY
            unit = min(p, NL)
            for c in range(2):
                v.full[...] = dot_tn(left[:, c * SN:(c + 1) * SN], right[...])
                for half, red in enumerate(pair):
                    cols = slice(half * (D // 2), (half + 1) * (D // 2))
                    for x in range(NX):
                        for part in range(NL // unit):
                            j = c * NL + part * unit
                            dst = ((j // p) * NX + x) * p + j % p if half else x * 2 * NL + j
                            mine = pl.ds(pl.multiple_of((x * 2 + core) * NL + part * unit, 8), unit)
                            theirs = pl.ds(pl.multiple_of((x * 2 + 1 - core) * NL + part * unit, 8), unit)
                            red.s[dst:dst + unit, :] = v.full[theirs, cols].astype(BF16)
                            red.own[dst:dst + unit, :] = v.full[mine, cols]
            for red in pair:
                red.start()

        def take_flat(dst):
            v.flat[0:FLAT, :] = v.raw[...].astype(F32)

            def body(s, c):
                for q in range(Q):
                    for j in range(LT):
                        part = v.flat[pl.ds(s * (LT * Q) + j * Q + q, CHUNKS, stride=ST * LT * Q), :]
                        dst[at_step(q, s), j * 128:(j + 1) * 128] = part.astype(BF16)
                return c

            lax.fori_loop(0, ST, body, 0)

        def put_flat(r, q, tile):
            for i in range(RT // CHUNKS):
                for j in range(LT):
                    v.flat[pl.ds((r // CHUNKS + i) * (LT * Q) + j * Q + q, CHUNKS, stride=ST * LT * Q), :] = (
                        tile[i * CHUNKS:(i + 1) * CHUNKS, j * 128:(j + 1) * 128])

        def weight(ref):
            return ref[...].reshape(SL2, D)

        def forward_tile(l, r):
            at = pl.ds(r, RT)
            u = read_u(l)(r)
            _, normed = normalise(l, u)
            mixed = dot_nn(v.slow[l][at, :], weight(v.wout[l]))
            x = mixed + skip_ref[l:l + 1, :] * normed
            x2 = x * x
            t = jnp.tanh(x * (GELU_A + (GELU_A * GELU_B) * x2))
            half = 0.5 * (1.0 + t)
            hidden = (x * half).astype(BF16)
            v.hid[l][at, :] = hidden
            dgelu = half + (0.5 * x) * (1.0 - t * t) * (GELU_A + (3.0 * GELU_A * GELU_B) * x2)
            both = dot_nn(hidden, v.wglu[l])
            linear = both[:, :D]
            gate = 0.5 + 0.5 * jnp.tanh(0.5 * both[:, D:])
            return u, normed, dgelu, linear, gate

        def backward_tile(l, r, upstream, normed, dgelu, linear, gate):
            at = pl.ds(r, RT)
            pass_gate = upstream * gate
            bothg = jnp.concatenate([pass_gate, pass_gate * linear * (1.0 - gate)], axis=1).astype(BF16)
            v.bothg[at, :] = bothg
            preg = dot_nt(bothg, v.wglu[l]) * dgelu
            v.preg[at, :] = preg
            mlow = preg.astype(BF16)
            v.mlow[at, :] = mlow
            v.sgrad[at, :] = dot_nt(mlow, weight(v.wout[l]))
            return fold8(preg * normed)

        def norm_grads(l, q, sums):
            def body(r, c):
                at = pl.ds(r + q * L, RT)
                standard, _ = normalise(l, read_u(l)(r + q * L))
                ng = v.preg[at, :] * skip_ref[l:l + 1, :] + dot_nn(v.mlow[at, :], weight(v.win[l]))
                v.preg[at, :] = ng
                return c[0] + fold8(ng), c[1] + fold8(ng * standard)
            return tiles(body, sums, TILES)

        def send_norm_grads(l, sums):
            msg, buf = v.bw_msg[l], v.bw_buf[l]
            msg[0:1, :] = fold1(sums[0])
            msg[1:2, :] = fold1(sums[1])
            buf[me] = msg[...]
            return send(ALL, msg, buf)

        def put_small(l, skip, chain):
            msg, r = v.sm_msg, 4 * l
            msg[r:r + 1, :] = fold1(skip)
            msg[r + 1:r + 2, 0:SN] = fold1(chain[0])
            msg[r + 1:r + 2, SN:] = fold1(chain[1])
            msg[r + 2:r + 3, 0:SN] = fold1(chain[2])
            msg[r + 2:r + 3, SN:] = jnp.zeros((1, SN), F32)
            msg[r + 3:r + 4, :] = jnp.zeros((1, D), F32)

        def send_small():
            v.sm_buf[me_t] = v.sm_msg[...]
            return send(STATE, v.sm_msg, v.sm_buf)

        def pass_small(got):
            got()
            v.sm_sum[...] = jnp.sum(v.sm_buf[...], axis=0)
            v.sm_all[me_s] = v.sm_sum[...]
            return send(SEQ, v.sm_sum, v.sm_all)

        def take_norm_grads(l, got):
            got()
            buf = v.bw_buf[l]
            total = jnp.sum(buf[...], axis=0)
            v.small[l][0:2, :] = total

        def take_small(got):
            got()
            total = jnp.sum(v.sm_all[...], axis=0)
            out = v.result
            out[...] = jnp.zeros((16, D), F32)

            def mine(row):
                held = jnp.zeros((1, NL), F32)
                for j in range(NT):
                    held = jnp.where(me_t == j, row[:, j * NL:(j + 1) * NL], held)
                return held

            for l in range(2):
                out[l:l + 1, :] = v.small[l][1:2, :]
                out[2 + l:3 + l, :] = v.small[l][0:1, :]
                out[4 + l:5 + l, :] = total[4 * l:4 * l + 1, :]
                sum_re = mine(total[4 * l + 1:4 * l + 2, 0:SN])
                sum_im = mine(total[4 * l + 1:4 * l + 2, SN:])
                sum_sc = mine(total[4 * l + 2:4 * l + 3, 0:SN])
                own = slice(l, l + 1)
                rate = jnp.exp(nu_ref[own, :])
                phase = jnp.exp(theta_ref[own, :])
                lre, lim = v.par_msg[3 * l:3 * l + 1, 0:NL], v.par_msg[3 * l + 1:3 * l + 2, 0:NL]
                slow = jnp.tanh(rate)
                root = jnp.sqrt(2.0 * slow / (1.0 + slow))
                rate_grad = sum_sc * gamma_ref[own, :] * jnp.exp(-2.0 * rate) / root - (sum_re * lre + sum_im * lim)
                out[6 + l:7 + l, 0:NL] = rate * rate_grad
                out[8 + l:9 + l, 0:NL] = phase * (sum_im * lre - sum_re * lim)
                out[10 + l:11 + l, 0:NL] = sum_sc * root

        def input_gradient(l, r, upstream):
            stat, small = v.stat[l], v.small[l]
            standard, _ = normalise(l, read_u(l)(r))
            m = rep(v.mask[pl.ds(r, RT), :])
            inner = small[0:1, :] + standard * small[1:2, :]
            ng = v.preg[pl.ds(r, RT), :] - m * inner / stat[2:3, :]
            return upstream + stat[1:2, :] * gain_ref[l:l + 1, :] * ng

        rate = jnp.exp(nu_ref[...])
        phase = jnp.exp(theta_ref[...])
        modulus = jnp.exp(-rate)
        lam_re, lam_im = modulus * jnp.cos(phase), modulus * jnp.sin(phase)
        slow = jnp.tanh(rate)
        root = jnp.sqrt(2.0 * slow / (1.0 + slow))
        scale_own = gamma_ref[...] * root
        v.par_msg[...] = jnp.zeros((8, 128), F32)
        v.len_msg[...] = jnp.zeros((8, 128), F32)
        for l in range(2):
            for i, row in enumerate((lam_re, lam_im, scale_own)):
                v.par_msg[3 * l + i:3 * l + i + 1, 0:NL] = row[l:l + 1, :]
        v.par_buf[me_t] = v.par_msg[...]
        for q in range(Q):
            v.len_msg[q:q + 1, :] = jnp.full((1, 128), 1.0, F32) * len_ref[q].astype(F32)
        v.len_buf[me_s] = v.len_msg[...]

        base = me_t * L
        row = lax.broadcasted_iota(jnp.int32, (L, 128), 0)
        token = base + lax.rem(row, CHUNKS) * ST + row // CHUNKS
        count_own = jnp.float32(0)
        for q in range(Q):
            v.mask[q * L:(q + 1) * L, :] = (token < len_ref[q]).astype(F32)
            count_own = count_own + jnp.clip(len_ref[q] - base, 0, L).astype(F32)

        got_x()
        take_flat(v.x0)
        got_cot = load(cot_hbm, v.raw)
        local_stats(read_u(0), 0)
        for wait in got_own:
            wait()
        pl.semaphore_wait(barrier, N - 1)
        got_len = send(SEQ, v.len_msg, v.len_buf)
        got = send(ALL, v.st_msg[0], v.st_buf[0])
        got_par = send(STATE, v.par_msg, v.par_buf)
        gathers = [[Gather(v.win[0])], []]
        got_par()
        v.par[...] = jnp.concatenate([v.par_buf[j, :, 0:NL] for j in range(NT)], axis=1)
        chunk_powers(0)
        chunk_powers(1)
        take_counts()
        gathers[0].append(Gather(v.wout[0]))
        gathers[0][0].relay()
        global_stats(0, got)
        gathers[0][1].relay()

        def project(l, q):
            def body(r, c):
                at = pl.ds(r + q * L, RT)
                _, normed = normalise(l, read_u(l)(r + q * L))
                low = normed.astype(BF16)
                v.nlow[l][at, :] = low
                v.proj[l][at, :] = dot_nt(low, weight(v.win[l]))
                return c
            tiles(body, 0, TILES)

        def forward_scan(l, between):
            gathers[l][0].take()
            waits = []
            for q in range(Q):
                project(l, q)
                waits.append(scan_ends(l, q))
            gathers[l][1].take()
            v.wout[l][1] = -v.wout[l][1]
            between()
            return waits

        def more_weights():
            gathers[1].append(Gather(v.win[1]))
            gathers[1].append(Gather(v.wout[1]))

        waits = forward_scan(0, lambda: None)
        got_glu()
        total = zero8
        for q in range(Q):
            scan_states(0, q, waits[q])
            if q == 0:
                more_weights()

            def body(r, acc, q=q):
                at = pl.ds(r + q * L, RT)
                u, normed, dgelu, linear, gate = forward_tile(0, r + q * L)
                v.dgelu[at, :] = dgelu
                v.lin[at, :] = linear
                v.gate[at, :] = gate
                u = u + linear * gate
                v.u1[at, :] = u
                return acc + fold8(u * rep(v.mask[at, :]))

            total = tiles(body, total, TILES)

        local_stats(read_u(1), 1, total)
        got = send(ALL, v.st_msg[1], v.st_buf[1])
        got_cot()
        take_flat(v.cot)
        gathers[1][0].relay()
        gathers[1][1].relay()
        global_stats(1, got)
        waits = forward_scan(1, lambda: None)
        skip = zero8
        waits_b = []
        for q in range(Q):
            scan_states(1, q, waits[q])

            def body(r, acc, q=q):
                at = pl.ds(r + q * L, RT)
                u, normed, dgelu, linear, gate = forward_tile(1, r + q * L)
                v.up[at, :] = u + linear * gate
                upstream = v.cot[at, :].astype(F32)
                return acc + backward_tile(1, r + q * L, upstream, normed, dgelu, linear, gate)

            skip = tiles(body, skip, TILES)
            waits_b.append(adjoint_ends(1, q))

        def advance(*which):
            for pair in which:
                for red in pair:
                    if red.stage < red.last:
                        red.step()

        def mixer_gradients(l, point):
            glu_gradient(l)
            advance(*plan[point])
            state_matrix_gradient(reducers[l][1], v.slow[l], v.mlow)
            advance(*plan[point + 1])

        def input_matrix_gradient(l):
            state_matrix_gradient(reducers[l][2], v.mlow, v.nlow[l])

        (g0, o0, i0), (g1, o1, i1) = reducers
        plan = [(), (g1,), (o1,), (), (g1,i1,o1,), (), (g1,o1,i1,), (), (), (g0,i1,), (), (o0,g1,o1,), (), (i0,g0,o0,i1,o1,g1,i1,), (), (g0,i0,g1,), (), ]
        stored = []

        mixer_gradients(1, 0)
        chain = (jnp.zeros((CHUNKS, SN), F32),) * 3
        sums = (zero8, zero8)
        for q in range(Q):
            chain = adjoint_states(1, q, waits_b[q], chain)
            sums = norm_grads(1, q, sums)
            if q == 0:
                advance(*plan[2])
        put_small(1, skip, chain)
        got = send_norm_grads(1, sums)
        input_matrix_gradient(1)
        advance(*plan[3])
        for q in range(Q):
            def body(r, c, q=q):
                put_flat(r, q, v.up[pl.ds(r + q * L, RT), :])
                return c
            tiles(body, 0, TILES)
        stored.append(load(v.flat.at[pl.ds(0, FLAT)], u2_out))
        advance(*plan[4])
        take_norm_grads(1, got)
        advance(*plan[5])

        skip = zero8
        waits_b = []
        for q in range(Q):
            def body(r, acc, q=q):
                at = pl.ds(r + q * L, RT)
                upstream = input_gradient(1, r + q * L, v.cot[at, :].astype(F32))
                v.up[at, :] = upstream
                _, normed = normalise(0, read_u(0)(r + q * L))
                return acc + backward_tile(0, r + q * L, upstream, normed, v.dgelu[at, :], v.lin[at, :], v.gate[at, :])

            skip = tiles(body, skip, TILES)
            waits_b.append(adjoint_ends(0, q))
            advance(*plan[6 + min(q, 1)])
        mixer_gradients(0, 8)
        chain = (jnp.zeros((CHUNKS, SN), F32),) * 3
        for q in range(Q):
            chain = adjoint_states(0, q, waits_b[q], chain)
        put_small(0, skip, chain)
        advance(*plan[10])
        input_matrix_gradient(0)
        got_small = send_small()
        advance(*plan[11])
        sums = (zero8, zero8)
        for q in range(Q):
            sums = norm_grads(0, q, sums)
            if q == 0:
                advance(*plan[12])
        got = send_norm_grads(0, sums)
        advance(*plan[13])
        take_norm_grads(0, got)
        advance(*plan[15])
        got_small = pass_small(got_small)
        stored[0]()

        for q in range(Q):
            def body(r, c, q=q):
                put_flat(r, q, input_gradient(0, r + q * L, v.up[pl.ds(r + q * L, RT), :]))
                return c

            tiles(body, 0, TILES)
        stored = [load(v.flat.at[pl.ds(0, FLAT)], ig_out)]
        advance(*plan[16])
        take_small(got_small)
        stored.append(load(v.result, small_out))
        order = [g0, i0, o0, g1, o1, i1]
        while any(pair[0].stage < pair[0].last for pair in order):
            for pair in order:
                advance(pair)
        for l in range(2):
            for half in range(2):
                stored.append(load(reducers[l][0][half].res, glu_out.at[l, half]))
                stored.append(load(reducers[l][1][half].res, out_out.at[l, half]))
                stored.append(load(reducers[l][2][half].res, int_out.at[l, half]))
        for w in pending:
            w()

    out_shape = [
        jax.ShapeDtypeStruct((FLAT, 128), F32),
        jax.ShapeDtypeStruct((FLAT, 128), F32),
        jax.ShapeDtypeStruct((16, D), F32),
        jax.ShapeDtypeStruct((2, 2, 2 * NL, D // 2), BF16),
        jax.ShapeDtypeStruct((2, 2, 2 * NL, D // 2), BF16),
        jax.ShapeDtypeStruct((2, 2, D, E // 2), BF16),
    ]
    hbm = pl.BlockSpec(memory_space=pl.ANY)
    vmem = pl.BlockSpec(memory_space=pltpu.VMEM)
    smem = pl.BlockSpec(memory_space=pltpu.SMEM)
    return pl.pallas_call(
        kernel,
        out_shape=out_shape,
        in_specs=[hbm, hbm, smem] + [vmem] * 6 + [hbm] * 3,
        out_specs=[hbm] * 6,
        scratch_shapes=scratch,
        compiler_params=pltpu.CompilerParams(
            collective_id=0, has_side_effects=True, vmem_limit_bytes=VMEM_LIMIT
        ),
    )


def finish(rows, seqs, width, own):
    D, NL = width, own
    FLAT = rows * seqs * D // 128

    def kernel(u2, ig, small, ing, outg, glu, u2_o, ig_o, gain_o, bias_o, skip_o, nu_o, theta_o, gamma_o, in_o, out_o, glu_o,
               wide, glu_low, glu_wide, in_low, out_low, in_wide, out_wide, sems):
        count = []

        def copy(src, dst):
            c = pltpu.make_async_copy(src, dst, sems.at[len(count)])
            count.append(c)
            c.start()
            return c

        got_glu = [copy(glu.at[l], glu_low.at[l]) for l in range(2)]
        got_u2, got_ig = copy(u2, wide.at[0]), copy(ig, wide.at[1])
        got_in, got_out = copy(ing, in_low), copy(outg, out_low)
        back = []
        for l in range(2):
            got_glu[l].wait()
            for half in range(2):
                glu_wide[l, :, half * D:(half + 1) * D] = glu_low[l, half].astype(F32)
            back.append(copy(glu_wide.at[l], glu_o.at[l]))
        got_u2.wait()
        back.append(copy(wide.at[0], u2_o))
        got_ig.wait()
        back.append(copy(wide.at[1], ig_o))
        got_in.wait()
        got_out.wait()
        for l in range(2):
            for half in range(2):
                cols = slice(half * (D // 2), (half + 1) * (D // 2))
                for c in range(2):
                    part = out_low[l, half, c * NL:(c + 1) * NL, :].astype(F32)
                    out_wide[l, c, :, cols] = -part if c else part
                    in_wide[l, c, :, cols] = in_low[l, half, c * NL:(c + 1) * NL, :].astype(F32)
        back += [copy(in_wide, in_o), copy(out_wide, out_o)]
        for l in range(2):
            for ref, at in ((gain_o, 0), (bias_o, 2), (skip_o, 4)):
                ref[l:l + 1, :] = small[at + l:at + l + 1, :]
            for ref, at in ((nu_o, 6), (theta_o, 8), (gamma_o, 10)):
                ref[l:l + 1, :] = small[at + l:at + l + 1, 0:NL]
        for b in back:
            b.wait()

    f32 = lambda *shape: jax.ShapeDtypeStruct(shape, F32)
    hbm = pl.BlockSpec(memory_space=pl.ANY)
    vmem = pl.BlockSpec(memory_space=pltpu.VMEM)
    return pl.pallas_call(
        kernel,
        out_shape=[f32(FLAT, 128), f32(FLAT, 128)] + [f32(2, D)] * 3 + [f32(2, NL)] * 3
        + [f32(2, 2, NL, D), f32(2, 2, NL, D), f32(2, D, 2 * D)],
        in_specs=[hbm, hbm, vmem] + [hbm] * 3,
        out_specs=[hbm, hbm] + [vmem] * 6 + [hbm] * 3,
        scratch_shapes=[
            pltpu.VMEM((2, FLAT, 128), F32),
            pltpu.VMEM((2, 2, D, D), BF16),
            pltpu.VMEM((2, D, 2 * D), F32),
            pltpu.VMEM((2, 2, 2 * NL, D // 2), BF16),
            pltpu.VMEM((2, 2, 2 * NL, D // 2), BF16),
            pltpu.VMEM((2, 2, NL, D), F32),
            pltpu.VMEM((2, 2, NL, D), F32),
            pltpu.SemaphoreType.DMA((12,)),
        ],
        compiler_params=pltpu.CompilerParams(vmem_limit_bytes=VMEM_LIMIT),
    )


def solution(mesh):
    seq_devices, state_devices = mesh.shape["seq"], mesh.shape["state"]

    def per_device(
        inputs, lengths, norm_gain, norm_bias, in_proj, out_proj,
        nu_log, theta_log, gamma_gain, skip_gain, glu_weight, cotangent,
    ):
        rows, seqs, width = inputs.shape
        layers, own = nu_log.shape
        lanes = width // 128

        def flat(a):
            a = a.reshape(rows, seqs, lanes, 128).transpose(0, 2, 1, 3)
            return a.reshape(rows * seqs * lanes, 128)

        def by_tokens(a):
            a = a.reshape(rows, lanes, seqs, 128).transpose(0, 2, 1, 3)
            return a.reshape(rows, seqs, width)

        step = build(seq_devices, state_devices, rows, seqs, width, own, layers)
        held = step(
            flat(inputs), flat(cotangent), lengths, norm_gain, norm_bias, nu_log, theta_log, gamma_gain, skip_gain,
            jnp.swapaxes(in_proj, 2, 3), out_proj, glu_weight,
        )
        u2, input_grad, gain, bias, skip, nu, theta, gamma, in_grad, out_grad, glu = finish(rows, seqs, width, own)(*held)
        return by_tokens(u2), by_tokens(input_grad), gain, bias, jnp.swapaxes(in_grad, 2, 3), out_grad, nu, theta, gamma, skip, glu

    return jax.shard_map(
        per_device,
        mesh=mesh,
        in_specs=(
            P("state", "seq", None),
            P("seq"),
            P(),
            P(),
            P(None, None, None, "state"),
            P(None, None, "state", None),
            P(None, "state"),
            P(None, "state"),
            P(None, "state"),
            P(),
            P(),
            P("state", "seq", None),
        ),
        out_specs=(
            P("state", "seq", None),
            P("state", "seq", None),
            P(),
            P(),
            P(None, None, None, "state"),
            P(None, None, "state", None),
            P(None, "state"),
            P(None, "state"),
            P(None, "state"),
            P(),
            P(),
        ),
        check_vma=False,
    )
```
